256 devices in a mesh: dp: 32 (over x, y, core), tensor: 8 (over z).
Axes of the slice: x: 4, y: 4, z: 8, core: 2. Of those that a mesh axis runs over, the one named last changes fastest.
Arguments:
- rotated_queries: bfloat16 [4096, 8192], P('dp', 'tensor'), may hold values from -5 to 5
- rotated_keys: bfloat16 [4096, 1024], P('dp', 'tensor'), may hold values from -5 to 5
- value_heads_packed: bfloat16 [4096, 1024], P('dp', 'tensor'), may hold values from -6 to 6
- out_weight: bfloat16 [8192, 4096], P('tensor'), may hold values from -0.0625 to 0.0625
- out_cotangent: bfloat16 [4096, 4096], P('dp', 'tensor'), may hold values from -6 to 6
- doc_ids: int32 [4096], P('dp'), may hold values from 0 to 15, never falling along the last dimension, each value on 1 to 2048 neighbouring positions
Outputs:
- projected: bfloat16 [4096, 4096], P('dp', 'tensor')
- query_grad: bfloat16 [4096, 8192], P('dp', 'tensor')
- key_state_gradient: bfloat16 [4096, 1024], P('dp', 'tensor')
- value_state_gradient: bfloat16 [4096, 1024], P('dp', 'tensor')
The draws below stay inside these ranges and needn't reach their ends.
Inputs may be any that keep to these rules, and one draw needn't show every extreme that they name: doc_ids never falls along the tokens; each number names one run of 1 to 2048 tokens, and one run has exactly 2048.
All inputs are finite; a program needn't handle non-finite values.
Results may differ from the reference program's by a relative error of at most 0.034.
Values may be sent and summed in bfloat16 or wider, within the bound.
No kernel may reach another device: no remote copies, remote signals or barrier semaphores. Data moves between devices by JAX's collectives and lax.ppermute only.
A program may use at most 128 MiB of HBM per device.

```python
import math
import jax
import jax.numpy as jnp
import numpy as np
from jax import lax

QUERY_HEAD_COUNT = 64
KEY_VALUE_HEADS = 8
HEAD_SIZE = 128
DW = 4096
TOK_DEV = 128
DOC_DEVS = 16
MAXLEN = 2048
DOCS = 16
TOKEN_TOTAL = 4096
N_TENSOR = 8


def draw_rotated_queries(key, part):
    key = jax.random.fold_in(key, 5)
    base_offset = jnp.clip(jax.random.normal(key, (TOKEN_TOTAL, QUERY_HEAD_COUNT, HEAD_SIZE), jnp.float32), -4.0, 4.0)
    return base_offset.reshape(TOKEN_TOTAL, QUERY_HEAD_COUNT * HEAD_SIZE).astype(jnp.bfloat16)


def draw_rotated_keys(key, part):
    key = jax.random.fold_in(key, 6)
    base_offset = jnp.clip(jax.random.normal(key, (TOKEN_TOTAL, KEY_VALUE_HEADS, HEAD_SIZE), jnp.float32), -4.0, 4.0)
    return base_offset.reshape(TOKEN_TOTAL, KEY_VALUE_HEADS * HEAD_SIZE).astype(jnp.bfloat16)


def steps_of(stream_key, shape, shards, low, high):
    level = 1.0
    for axis_at, shards_of in shards:
        heights = jax.random.uniform(jax.random.fold_in(jax.random.fold_in(stream_key, 6), axis_at), (shards_of,), jnp.float32, low / len(shards), high / len(shards))
        level = level * jnp.repeat(jnp.exp(heights), shape[axis_at] // shards_of).reshape((-1,) + (1,) * (len(shape) - 1 - axis_at))
    return level


def profile(amount, total, reach, skew):
    loads = [(1 << 20) // math.isqrt(standing ** skew) + 1 for standing in range(2, amount + 1)]
    rest, holding = total - reach - (amount - 1), [1] * (amount - 1)
    while rest > 0:
        free = [i for i in range(amount - 1) if holding[i] < reach]
        mass, remaining = sum([loads[i] for i in free]), rest
        for i in free:
            more = min(reach - holding[i], max(1, remaining * loads[i] // mass), rest)
            holding[i] = holding[i] + more
            rest = rest - more
    return np.array([reach] + holding)


def ragged(stream_key, number_of, total, limit, skew):
    if number_of == 2:
        one = jax.random.randint(stream_key, (), max(1, total - limit), min(limit, total - 1) + 1)
        return jnp.stack([one, total - one])
    sizes = jnp.asarray(profile(number_of, total, limit, skew), jnp.int32)
    pairs = (number_of - 1) // 2
    source_of, receiver = sizes[1:1 + 2 * pairs:2], sizes[2:2 + 2 * pairs:2]
    slack = jnp.minimum(source_of - 1, limit - receiver)
    moved = jax.random.randint(jax.random.fold_in(stream_key, 1), (pairs,), 0, 1 << 20) % (slack + 1)
    sizes = sizes.at[1:1 + 2 * pairs:2].set(source_of - moved).at[2:2 + 2 * pairs:2].set(receiver + moved)
    return sizes[jax.random.permutation(jax.random.fold_in(stream_key, 2), number_of)]


def centred(key, extent, width, bound, split=(), held_as=jnp.bfloat16):
    loudness = steps_of(key, extent, split, -0.22, 0.18) if split else 1.0
    drawn = jax.random.normal(key, extent, jnp.float32) * width * loudness
    return jnp.minimum(jnp.maximum(drawn, -bound), bound).astype(held_as)


def setup_inputs(seed: int = 0) -> dict:
    streams_of = jax.random.split(jax.random.key(seed), 7)
    return {
        "rotated_queries": draw_rotated_queries(jax.random.fold_in(streams_of[6], 71), 0),
        "rotated_keys": draw_rotated_keys(jax.random.fold_in(streams_of[6], 71), 0),
        "value_heads_packed": centred(streams_of[2], (TOKEN_TOTAL, KEY_VALUE_HEADS * HEAD_SIZE), 1.0, 6.0, ((0, 32), (1, 8))),
        "out_weight": centred(streams_of[3], (QUERY_HEAD_COUNT * HEAD_SIZE, DW), (QUERY_HEAD_COUNT * HEAD_SIZE) ** -0.5, 0.0625, ((0, 8),)),
        "out_cotangent": centred(streams_of[4], (TOKEN_TOTAL, DW), 1.0, 6.0, ((0, 32), (1, 8))),
        "doc_ids": jnp.searchsorted(jnp.cumsum(ragged(streams_of[5], DOCS, TOKEN_TOTAL, MAXLEN, 2)), jnp.arange(TOKEN_TOTAL), side="right").astype(jnp.int32),
    }


masked_score = -1e+30

def scores_for(query_heads, key_blk, allowed):
    raw_scores = jnp.einsum('cgtd,scd->cgts', query_heads, key_blk)
    return jnp.where(allowed, raw_scores * (1.0 / math.sqrt(HEAD_SIZE)), masked_score)

def no_scores(query_heads, key_blk, allowed):
    return jnp.full(query_heads.shape[:3] + (key_blk.shape[0],), masked_score, jnp.float32)

def mix_values(weight, value_blk):
    low_weight = lax.optimization_barrier(weight.astype(jnp.bfloat16)).astype(jnp.float32)
    return jnp.einsum('cgts,scd->cgtd', low_weight, value_blk)

def no_mix(weight, value_blk):
    return jnp.zeros(weight.shape[:3] + (value_blk.shape[-1],), jnp.float32)

def grad_terms(score_blk, key_blk, value_blk, query_heads, grad_heads, log_total, row_delta):
    probability = jnp.exp(score_blk - log_total[..., None])
    low_prob = lax.optimization_barrier(probability.astype(jnp.bfloat16)).astype(jnp.float32)
    value_term = jnp.einsum('cgts,cgtd->scd', low_prob, grad_heads)
    grad_prob = jnp.einsum('cgtd,scd->cgts', grad_heads, value_blk)
    grad_score = probability * (grad_prob - row_delta[..., None]) * (1.0 / math.sqrt(HEAD_SIZE))
    grad_score = lax.optimization_barrier(grad_score.astype(jnp.bfloat16)).astype(jnp.float32)
    query_term = jnp.einsum('cgts,scd->cgtd', grad_score, key_blk)
    key_term = jnp.einsum('cgts,cgtd->scd', grad_score, query_heads)
    return (query_term, key_term, value_term)

def no_terms(score_blk, key_blk, value_blk, query_heads, grad_heads, log_total, row_delta):
    zero_rows = jnp.zeros(key_blk.shape, jnp.float32)
    return (jnp.zeros(query_heads.shape, jnp.float32), zero_rows, zero_rows)

def reference(rotated_queries, rotated_keys, value_heads_packed, out_weight, out_cotangent, doc_ids):
    query_group_width = QUERY_HEAD_COUNT // KEY_VALUE_HEADS
    row_count = TOK_DEV
    reach_devs = DOC_DEVS
    slack_margin = reach_devs * row_count
    gathered_queries = rotated_queries.reshape(TOKEN_TOTAL, KEY_VALUE_HEADS, query_group_width, HEAD_SIZE)
    gathered_keys = jnp.concatenate([jnp.zeros((slack_margin, KEY_VALUE_HEADS, HEAD_SIZE), rotated_keys.dtype), rotated_keys.reshape(TOKEN_TOTAL, KEY_VALUE_HEADS, HEAD_SIZE)], 0)
    gathered_values = jnp.concatenate([jnp.zeros((slack_margin, KEY_VALUE_HEADS, HEAD_SIZE), value_heads_packed.dtype), value_heads_packed.reshape(TOKEN_TOTAL, KEY_VALUE_HEADS, HEAD_SIZE)], 0)
    id_all = jnp.concatenate([jnp.full((slack_margin,), -1, jnp.int32), doc_ids.astype(jnp.int32)], 0)
    attended_gradient = jnp.dot(out_cotangent, out_weight.T, preferred_element_type=jnp.float32).astype(jnp.bfloat16)
    gradient_total = attended_gradient.reshape(TOKEN_TOTAL, KEY_VALUE_HEADS, query_group_width, HEAD_SIZE)

    def one_block(gradient_sums, block_index):
        key_sum, value_sum = gradient_sums
        first_row = block_index * row_count
        query_heads = jnp.transpose(lax.dynamic_slice_in_dim(gathered_queries, first_row, row_count, 0), (1, 2, 0, 3)).astype(jnp.float32)
        grad_heads = jnp.transpose(lax.dynamic_slice_in_dim(gradient_total, first_row, row_count, 0), (1, 2, 0, 3)).astype(jnp.float32)
        query_ids = lax.dynamic_slice_in_dim(doc_ids.astype(jnp.int32), first_row, row_count, 0)
        query_pos = first_row + jnp.arange(row_count, dtype=jnp.int32)
        pieces = []
        for distance in range(reach_devs + 1):
            key_start = (first_row + slack_margin - distance * row_count).astype(jnp.int32)
            key_blk = lax.dynamic_slice_in_dim(gathered_keys, key_start, row_count, 0).astype(jnp.float32)
            value_blk = lax.dynamic_slice_in_dim(gathered_values, key_start, row_count, 0).astype(jnp.float32)
            key_ids = lax.dynamic_slice_in_dim(id_all, key_start, row_count, 0)
            key_pos = key_start - slack_margin + jnp.arange(row_count, dtype=jnp.int32)
            allowed = (query_ids[:, None] == key_ids[None, :]) & (key_pos[None, :] <= query_pos[:, None])
            live_flag = jnp.any(allowed)
            scores = lax.cond(live_flag, scores_for, no_scores, query_heads, key_blk, allowed)
            pieces.append((key_start, key_blk, value_blk, live_flag, scores))
        row_peak = lax.optimization_barrier(jnp.max(jnp.stack([lax.optimization_barrier(jnp.max(record[4], axis=-1)) for record in pieces]), axis=0))
        row_total = jnp.zeros(query_heads.shape[:3], jnp.float32)
        weighted = jnp.zeros(query_heads.shape, jnp.float32)
        for record in pieces:
            weight = jnp.exp(record[4] - row_peak[..., None])
            row_total = row_total + lax.optimization_barrier(jnp.sum(weight, axis=-1))
            weighted = weighted + lax.cond(record[3], mix_values, no_mix, weight, record[2])
        attended = (weighted / row_total[..., None]).astype(jnp.bfloat16)
        log_total = row_peak + jnp.log(row_total)
        row_delta = lax.optimization_barrier(jnp.sum(grad_heads * attended.astype(jnp.float32), axis=-1))
        query_sum = jnp.zeros(query_heads.shape, jnp.float32)
        for record in pieces:
            terms = lax.cond(record[3], grad_terms, no_terms, record[4], record[1], record[2], query_heads, grad_heads, log_total, row_delta)
            query_sum = query_sum + terms[0]
            old_keys = lax.dynamic_slice_in_dim(key_sum, record[0], row_count, 0)
            key_sum = lax.dynamic_update_slice_in_dim(key_sum, old_keys + terms[1], record[0], 0)
            old_values = lax.dynamic_slice_in_dim(value_sum, record[0], row_count, 0)
            value_sum = lax.dynamic_update_slice_in_dim(value_sum, old_values + terms[2], record[0], 0)
        attended_rows = jnp.transpose(attended, (2, 0, 1, 3)).reshape(row_count, QUERY_HEAD_COUNT * HEAD_SIZE)
        query_rows = jnp.transpose(query_sum, (2, 0, 1, 3)).reshape(row_count, QUERY_HEAD_COUNT * HEAD_SIZE).astype(jnp.bfloat16)
        return ((key_sum, value_sum), (attended_rows, query_rows))
    empty_gradients = jnp.zeros((slack_margin + TOKEN_TOTAL, KEY_VALUE_HEADS, HEAD_SIZE), jnp.float32)
    gradient_sums, stacked = lax.scan(one_block, (empty_gradients, empty_gradients), jnp.arange(TOKEN_TOTAL // TOK_DEV, dtype=jnp.int32))
    attended_all = stacked[0].reshape(TOKEN_TOTAL, QUERY_HEAD_COUNT * HEAD_SIZE)
    query_grad = stacked[1].reshape(TOKEN_TOTAL, QUERY_HEAD_COUNT * HEAD_SIZE)
    head_cols = QUERY_HEAD_COUNT * HEAD_SIZE // N_TENSOR
    projected = jnp.zeros((TOKEN_TOTAL, DW), jnp.float32)
    for shard_index in range(N_TENSOR):
        lower = shard_index * head_cols
        partial_out = jnp.dot(attended_all[:, lower:lower + head_cols], out_weight[lower:lower + head_cols], preferred_element_type=jnp.float32)
        projected = projected + lax.optimization_barrier(partial_out.astype(jnp.bfloat16)).astype(jnp.float32)
    key_state_gradient = gradient_sums[0][slack_margin:].reshape(TOKEN_TOTAL, KEY_VALUE_HEADS * HEAD_SIZE).astype(jnp.bfloat16)
    value_state_gradient = gradient_sums[1][slack_margin:].reshape(TOKEN_TOTAL, KEY_VALUE_HEADS * HEAD_SIZE).astype(jnp.bfloat16)
    return (projected.astype(jnp.bfloat16), query_grad, key_state_gradient, value_state_gradient)
```

```python
import functools
import math

import jax
import jax.numpy as jnp
from jax import lax
from jax.experimental import pallas as pl
from jax.experimental.pallas import tpu as pltpu
from jax.sharding import PartitionSpec as P

HEADS = 8
HEAD_SIZE = 128
TOK = 128
PAIR = 2 * TOK
DOCS = 16
ROWS = TOK + DOCS
SLOTS = 9
DIAGONAL = 2
CHUNK = 256
QROWS = HEADS * TOK
FEATURES = 512
MASKED = -1e30
SCALE = 1.0 / math.sqrt(HEAD_SIZE)
SCALE_LOG2 = SCALE * math.log2(math.e)

VMEM = pl.BlockSpec(memory_space=pltpu.VMEM)
SMEM = pl.BlockSpec(memory_space=pltpu.SMEM)
NT = (((1,), (1,)), ((), ()))
TN = (((0,), (0,)), ((), ()))


def dot_nt(a, b):
    return lax.dot_general(a, b, NT, preferred_element_type=jnp.float32)


def dot_tn(a, b):
    return lax.dot_general(a, b, TN, preferred_element_type=jnp.float32)


def dot(a, b):
    return jnp.dot(a, b, preferred_element_type=jnp.float32)


def params(mib=32):
    return pltpu.CompilerParams(vmem_limit_bytes=mib * 1024 * 1024)


def cost(flops, nbytes, trans=0):
    return pl.CostEstimate(flops=flops, bytes_accessed=nbytes, transcendentals=trans)


def pack_kernel(key_ref, value_ref, id_ref, out_ref):
    out_ref[0:TOK, 0:HEAD_SIZE] = key_ref[...]
    out_ref[0:TOK, HEAD_SIZE : 2 * HEAD_SIZE] = value_ref[...]
    number = lax.broadcasted_iota(jnp.int32, (DOCS, TOK), 0)
    below = jnp.where(id_ref[...] < number, 1.0, 0.0)
    count = jnp.sum(below, axis=1, keepdims=True)
    out_ref[TOK:ROWS, :] = jnp.broadcast_to(count, (DOCS, 2 * HEAD_SIZE)).astype(jnp.bfloat16)


def pick_kernel(info_ref, p0_ref, p1_ref, p2_ref, *out_refs):
    for n, out_ref in enumerate(out_refs):
        near = info_ref[n] == 1

        @pl.when(near)
        def _():
            out_ref[0] = p1_ref[...]
            out_ref[1] = p0_ref[...]

        @pl.when(jnp.logical_not(near))
        def _():
            out_ref[0] = p2_ref[...]
            out_ref[1] = p1_ref[...]


def pair_of(own_ref, sib_ref, slot, lower):
    cols = slice(lower, lower + HEAD_SIZE)
    return jnp.concatenate([own_ref[slot, 0:TOK, cols], sib_ref[slot, 0:TOK, cols]], 0)


def bias_of(pair, core, query_pair, first_row):
    row = lax.broadcasted_iota(jnp.int32, (PAIR, TOK), 0)
    column = lax.broadcasted_iota(jnp.int32, (PAIR, TOK), 1)
    shift = jnp.where(row < TOK, core * TOK, -core * TOK)
    key_pos = pair * PAIR + row + shift
    query_pos = query_pair * PAIR + core * TOK + column
    allowed = (key_pos >= first_row) & (key_pos <= query_pos)
    bias = jnp.where(allowed, 0.0, MASKED)
    return jnp.concatenate([bias] * (CHUNK // TOK), 1)


def split_heads(source_ref, rows_ref):
    for h in range(HEADS):
        rows_ref[h * TOK : (h + 1) * TOK, :] = source_ref[:, h * HEAD_SIZE : (h + 1) * HEAD_SIZE]


def forward_kernel(
    info_ref, q_ref, id_ref, own_ref, sib_ref, att_ref, log_ref, first_ref, rows_ref, acc_ref, max_ref, sum_ref
):
    query_pair, core = info_ref[SLOTS], info_ref[SLOTS + 1]
    split_heads(q_ref, rows_ref)
    below = jnp.zeros((DOCS, TOK), jnp.float32)
    for s in range(SLOTS):
        valid = jnp.where(info_ref[s] >= 0, 1.0, 0.0)
        counts = own_ref[s, TOK:ROWS, 0:TOK].astype(jnp.float32) + sib_ref[s, TOK:ROWS, 0:TOK].astype(jnp.float32)
        below = below + valid * counts
    number = lax.broadcasted_iota(jnp.int32, (DOCS, TOK), 0)
    before = jnp.sum(jnp.where(id_ref[...] == number, below, 0.0), axis=0, keepdims=True)
    first_row = before.astype(jnp.int32) + PAIR * jnp.maximum(query_pair - (SLOTS - 1), 0)
    first_ref[...] = first_row
    earliest = jnp.min(first_row)
    max_ref[...] = jnp.full(max_ref.shape, MASKED, jnp.float32)
    sum_ref[...] = jnp.zeros(sum_ref.shape, jnp.float32)
    acc_ref[...] = jnp.zeros(acc_ref.shape, jnp.float32)

    def attend(slot, pair):
        key = pair_of(own_ref, sib_ref, slot, 0)
        value = pair_of(own_ref, sib_ref, slot, HEAD_SIZE)
        bias = bias_of(pair, core, query_pair, first_row)
        for n in range(QROWS // CHUNK):
            cols = slice(n * CHUNK, (n + 1) * CHUNK)
            score = dot_nt(key, rows_ref[cols, :]) * SCALE_LOG2 + bias
            old = max_ref[:, cols]
            new = jnp.maximum(old, jnp.max(score, axis=0, keepdims=True))
            weight = jnp.exp2(score - new)
            fade = jnp.exp2(old - new)
            max_ref[:, cols] = new
            sum_ref[:, cols] = sum_ref[:, cols] * fade + jnp.sum(weight, axis=0, keepdims=True)
            acc_ref[:, cols] = acc_ref[:, cols] * fade + dot_tn(value, weight.astype(jnp.bfloat16))

    attend(DIAGONAL, query_pair)

    def step(slot, unused):
        pair = info_ref[slot]
        live = (pair >= 0) & (pair * PAIR + PAIR - 1 >= earliest) & (slot != DIAGONAL)

        @pl.when(live)
        def _():
            attend(slot, pair)

        return unused

    lax.fori_loop(0, SLOTS, step, 0)
    log_ref[...] = max_ref[...] + jnp.log2(sum_ref[...])
    for h in range(HEADS):
        cols = slice(h * TOK, (h + 1) * TOK)
        mixed = acc_ref[:, cols] / sum_ref[:, cols]
        att_ref[:, h * HEAD_SIZE : (h + 1) * HEAD_SIZE] = mixed.T.astype(jnp.bfloat16)


def backward_kernel(
    info_ref,
    q_ref,
    own_ref,
    sib_ref,
    att_ref,
    grad_ref,
    log_ref,
    first_ref,
    dq_ref,
    down_ref,
    dsib_ref,
    rows_ref,
    grows_ref,
    acc_ref,
    delta_ref,
):
    query_pair, core = info_ref[SLOTS], info_ref[SLOTS + 1]
    split_heads(q_ref, rows_ref)
    split_heads(grad_ref, grows_ref)
    first_row = first_ref[...]
    earliest = jnp.min(first_row)
    for h in range(HEADS):
        cols = slice(h * HEAD_SIZE, (h + 1) * HEAD_SIZE)
        product = grad_ref[:, cols].astype(jnp.float32) * att_ref[:, cols].astype(jnp.float32)
        delta_ref[:, h * TOK : (h + 1) * TOK] = jnp.sum(product.T, axis=0, keepdims=True)
    acc_ref[...] = jnp.zeros(acc_ref.shape, jnp.float32)

    def step(slot, unused):
        pair = info_ref[slot]
        live = (pair >= 0) & (pair * PAIR + PAIR - 1 >= earliest)

        @pl.when(live)
        def _():
            key = pair_of(own_ref, sib_ref, slot, 0)
            value = pair_of(own_ref, sib_ref, slot, HEAD_SIZE)
            bias = bias_of(pair, core, query_pair, first_row)
            dkey = jnp.zeros((PAIR, HEAD_SIZE), jnp.float32)
            dvalue = jnp.zeros((PAIR, HEAD_SIZE), jnp.float32)
            for n in range(QROWS // CHUNK):
                cols = slice(n * CHUNK, (n + 1) * CHUNK)
                score = dot_nt(key, rows_ref[cols, :]) * SCALE_LOG2 + bias
                prob = jnp.exp2(score - log_ref[:, cols])
                gprob = dot_nt(value, grows_ref[cols, :])
                gscore = (prob * (gprob - delta_ref[:, cols])).astype(jnp.bfloat16)
                dvalue = dvalue + dot(prob.astype(jnp.bfloat16), grows_ref[cols, :])
                dkey = dkey + dot(gscore, rows_ref[cols, :])
                acc_ref[:, cols] = acc_ref[:, cols] + dot_tn(key, gscore)
            dkey = (dkey * SCALE).astype(jnp.bfloat16)
            dvalue = dvalue.astype(jnp.bfloat16)
            for ref, rows in ((down_ref, slice(0, TOK)), (dsib_ref, slice(TOK, PAIR))):
                ref[slot, :, 0:HEAD_SIZE] = dkey[rows]
                ref[slot, :, HEAD_SIZE : 2 * HEAD_SIZE] = dvalue[rows]

        @pl.when(jnp.logical_not(live))
        def _():
            zero = jnp.zeros((TOK, 2 * HEAD_SIZE), jnp.bfloat16)
            down_ref[slot] = zero
            dsib_ref[slot] = zero

        return unused

    lax.fori_loop(0, SLOTS, step, 0)
    for h in range(HEADS):
        mixed = acc_ref[:, h * TOK : (h + 1) * TOK] * SCALE
        dq_ref[:, h * HEAD_SIZE : (h + 1) * HEAD_SIZE] = mixed.T.astype(jnp.bfloat16)


def core_sum_kernel(own_ref, arrived_ref, column_ref, minus_ref, plus_ref, two_ref):
    def total(s):
        return own_ref[s].astype(jnp.float32) + arrived_ref[s].astype(jnp.float32)

    for s in range(3):
        column_ref[s] = total(s)
    for n, ref in enumerate((minus_ref, plus_ref, two_ref)):
        for j in range(2):
            ref[j] = total(3 + 2 * n + j).astype(jnp.bfloat16)


def column_sum_kernel(info_ref, column_ref, a_ref, b_ref, c_ref, keep_ref, one_ref, two_ref, sum_ref):
    sum_ref[...] = column_ref[...]
    for n, ref in enumerate((a_ref, b_ref, c_ref)):
        for j in range(2):
            at = info_ref[n] + j
            sum_ref[at] = sum_ref[at] + ref[j].astype(jnp.float32)
    keep_ref[...] = sum_ref[2]
    one_ref[...] = sum_ref[1].astype(jnp.bfloat16)
    two_ref[...] = sum_ref[0].astype(jnp.bfloat16)


def project_kernel(at_ref, att_ref, w_ref, *out_refs):
    product = dot(att_ref[...], w_ref[...])
    for n, ref in enumerate(out_refs):
        for j in range(ref.shape[0]):

            @pl.when(pl.program_id(0) == n * ref.shape[0] + j)
            def _():
                ref[j] = product.astype(ref.dtype)


def project(at, attended, out_weight, outs):
    steps = sum(o.shape[0] for o in outs)
    whole = lambda shape: pl.BlockSpec(shape, lambda n, at: (0,) * len(shape))
    return pl.pallas_call(
        project_kernel,
        grid_spec=pltpu.PrefetchScalarGridSpec(
            num_scalar_prefetch=1,
            grid=(steps,),
            in_specs=[
                whole(attended.shape),
                pl.BlockSpec((QROWS, FEATURES), lambda n, at: (0, at[n])),
            ],
            out_specs=[whole(o.shape) for o in outs],
        ),
        out_shape=outs,
        compiler_params=params(),
        cost_estimate=cost(2 * steps * TOK * QROWS * FEATURES, steps * QROWS * FEATURES * 2),
    )(at, attended, out_weight)


def cotangent_kernel(blocks, has_start, at_ref, *refs):
    pieces, refs = refs[:blocks], refs[blocks:]
    if has_start:
        start_ref, w_ref, out_ref, acc_ref = refs
    else:
        w_ref, out_ref, acc_ref = refs
    n = pl.program_id(0)

    @pl.when(n == 0)
    def _():
        acc_ref[...] = start_ref[...] if has_start else jnp.zeros(acc_ref.shape, jnp.float32)

    at = 0
    for ref in pieces:
        for j in range(ref.shape[0] // TOK):

            @pl.when(n == at)
            def _():
                acc_ref[...] += dot_nt(ref[j * TOK : (j + 1) * TOK, :], w_ref[...])

            at = at + 1

    @pl.when(n == at - 1)
    def _():
        out_ref[...] = acc_ref[...].astype(out_ref.dtype)


def cotangent(at, pieces, start, out_weight, dtype):
    steps = sum(p.shape[0] for p in pieces) // TOK
    whole = lambda shape: pl.BlockSpec(shape, lambda n, at: (0,) * len(shape))
    operands = list(pieces) + ([] if start is None else [start])
    return pl.pallas_call(
        functools.partial(cotangent_kernel, len(pieces), start is not None),
        grid_spec=pltpu.PrefetchScalarGridSpec(
            num_scalar_prefetch=1,
            grid=(steps,),
            in_specs=[whole(o.shape) for o in operands]
            + [pl.BlockSpec((QROWS, FEATURES), lambda n, at: (0, at[n]))],
            out_specs=whole((TOK, QROWS)),
            scratch_shapes=[pltpu.VMEM((TOK, QROWS), jnp.float32)],
        ),
        out_shape=jax.ShapeDtypeStruct((TOK, QROWS), dtype),
        compiler_params=params(),
        cost_estimate=cost(2 * steps * TOK * QROWS * FEATURES, steps * QROWS * FEATURES * 2),
    )(at, *operands, out_weight)


def dp_of(x, y, c):
    return (x % 4) * 8 + (y % 4) * 2 + c


PLACES = [(x, y, c) for x in range(4) for y in range(4) for c in range(2)]


def along_x(value, by):
    return lax.ppermute(value, "dp", [(dp_of(x, y, c), dp_of(x + by, y, c)) for x, y, c in PLACES])


def along_y(value, by):
    return lax.ppermute(value, "dp", [(dp_of(x, y, c), dp_of(x, y + by, c)) for x, y, c in PLACES])


def across(value):
    return lax.ppermute(value, "dp", [(i, i ^ 1) for i in range(32)])


def along_z(value, by):
    return lax.ppermute(value, "tensor", [(i, (i + by) % 8) for i in range(8)])


def shaped(*shape, dtype=jnp.bfloat16):
    return jax.ShapeDtypeStruct(shape, dtype)


def per_device(rotated_queries, rotated_keys, value_heads_packed, out_weight, out_cotangent, doc_ids):
    me = lax.axis_index("dp").astype(jnp.int32)
    z = lax.axis_index("tensor").astype(jnp.int32)
    x, y, core = me // 8, (me // 2) % 4, me % 2
    pairs = [(x - 2) * 4 + y, (x - 1) * 4 + y, x * 4 + y]
    for by in (-1, 1, 2):
        other = (y + by) % 4
        row = x - 2 + (other < y).astype(jnp.int32)
        pairs += [row * 4 + other, (row + 1) * 4 + other]
    info = jnp.stack(pairs + [x * 4 + y, core])
    ahead = jnp.stack([y != 3, y == 0, y < 2]).astype(jnp.int32)
    ids = doc_ids.reshape(1, TOK)

    z_near = [along_z(out_cotangent, -1), along_z(out_cotangent, 1), along_z(out_cotangent, 4)]
    block = pl.pallas_call(
        pack_kernel, in_specs=[VMEM] * 3, out_specs=VMEM, out_shape=shaped(ROWS, 2 * HEAD_SIZE)
    )(rotated_keys, value_heads_packed, ids)
    block_1 = along_x(block, 1)
    block_2 = along_x(block, 2)
    send_up, send_down, send_two = pl.pallas_call(
        pick_kernel,
        in_specs=[SMEM] + [VMEM] * 3,
        out_specs=[VMEM] * 3,
        out_shape=[shaped(2, ROWS, 2 * HEAD_SIZE)] * 3,
    )(ahead, block, block_1, block_2)
    from_minus = along_y(send_up, 1)
    from_plus = along_y(send_down, -1)
    from_two = along_y(send_two, 2)
    own = jnp.concatenate([block_2[None], block_1[None], block[None], from_minus, from_plus, from_two], 0)
    sib = across(own)

    z_far_up = along_z(jnp.concatenate([z_near[0], z_near[2]], 0), -1)
    z_far_down = along_z(jnp.concatenate([z_near[1], z_near[2]], 0), 1)

    attention_flops = 2 * SLOTS * PAIR * QROWS * HEAD_SIZE
    attended, log_total, first_row = pl.pallas_call(
        forward_kernel,
        in_specs=[SMEM] + [VMEM] * 4,
        out_specs=[VMEM] * 3,
        out_shape=[
            shaped(TOK, QROWS),
            shaped(1, QROWS, dtype=jnp.float32),
            shaped(1, TOK, dtype=jnp.int32),
        ],
        scratch_shapes=[
            pltpu.VMEM((QROWS, HEAD_SIZE), jnp.bfloat16),
            pltpu.VMEM((HEAD_SIZE, QROWS), jnp.float32),
            pltpu.VMEM((1, QROWS), jnp.float32),
            pltpu.VMEM((1, QROWS), jnp.float32),
        ],
        compiler_params=params(),
        cost_estimate=cost(2 * attention_flops, 4 << 20, SLOTS * PAIR * QROWS),
    )(info, rotated_queries, ids, own, sib)

    grad_near = cotangent(
        (z + jnp.array([0, 1, 7, 4], jnp.int32)) % 8, [out_cotangent] + z_near, None, out_weight, jnp.float32
    )
    attended_gradient = cotangent(
        (z + jnp.array([2, 5, 6, 3], jnp.int32)) % 8, [z_far_up, z_far_down], grad_near, out_weight, jnp.bfloat16
    )

    to_up, to_down = project(
        (z + jnp.array([2, 5, 6, 3], jnp.int32)) % 8, attended, out_weight, [shaped(2, TOK, FEATURES)] * 2
    )
    got_up = along_z(to_up, 1)
    got_down = along_z(to_down, -1)
    near_up, near_four, near_down, kept = project(
        (z + jnp.array([1, 4, 7, 0], jnp.int32)) % 8,
        attended,
        out_weight,
        [shaped(1, TOK, FEATURES, dtype=jnp.float32)] * 4,
    )
    wide = lambda v: v.astype(jnp.float32)
    low = lambda v: v.astype(jnp.bfloat16)
    sum_up = along_z(low(near_up[0] + wide(got_up[0])), 1)
    sum_four = along_z(low(near_four[0] + wide(got_up[1]) + wide(got_down[1])), 4)
    sum_down = along_z(low(near_down[0] + wide(got_down[0])), -1)
    projected = low(kept[0] + wide(sum_up) + wide(sum_four) + wide(sum_down))

    query_grad, grad_own, grad_sib = pl.pallas_call(
        backward_kernel,
        in_specs=[SMEM] + [VMEM] * 7,
        out_specs=[VMEM] * 3,
        out_shape=[
            shaped(TOK, QROWS),
            shaped(SLOTS, TOK, 2 * HEAD_SIZE),
            shaped(SLOTS, TOK, 2 * HEAD_SIZE),
        ],
        scratch_shapes=[
            pltpu.VMEM((QROWS, HEAD_SIZE), jnp.bfloat16),
            pltpu.VMEM((QROWS, HEAD_SIZE), jnp.bfloat16),
            pltpu.VMEM((HEAD_SIZE, QROWS), jnp.float32),
            pltpu.VMEM((1, QROWS), jnp.float32),
        ],
        compiler_params=params(),
        cost_estimate=cost(5 * attention_flops, 5 << 20, SLOTS * PAIR * QROWS),
    )(info, rotated_queries, own, sib, attended, attended_gradient, log_total, first_row)

    arrived = across(grad_sib)
    column, to_minus, to_plus, to_two = pl.pallas_call(
        core_sum_kernel,
        in_specs=[VMEM] * 2,
        out_specs=[VMEM] * 4,
        out_shape=[shaped(3, TOK, 2 * HEAD_SIZE, dtype=jnp.float32)] + [shaped(2, TOK, 2 * HEAD_SIZE)] * 3,
    )(grad_own, arrived)
    back_a = along_y(to_minus, -1)
    back_b = along_y(to_plus, 1)
    back_c = along_y(to_two, 2)
    keep, one_back, two_back = pl.pallas_call(
        column_sum_kernel,
        in_specs=[SMEM] + [VMEM] * 4,
        out_specs=[VMEM] * 3,
        out_shape=[shaped(TOK, 2 * HEAD_SIZE, dtype=jnp.float32)] + [shaped(TOK, 2 * HEAD_SIZE)] * 2,
        scratch_shapes=[pltpu.VMEM((3, TOK, 2 * HEAD_SIZE), jnp.float32)],
    )(ahead, column, back_a, back_b, back_c)
    total = keep + wide(along_x(one_back, -1)) + wide(along_x(two_back, -2))
    total = low(total)
    return projected, query_grad, total[:, :HEAD_SIZE], total[:, HEAD_SIZE:]


def solution(mesh):
    return jax.shard_map(
        per_device,
        mesh=mesh,
        in_specs=(
            P("dp", "tensor"),
            P("dp", "tensor"),
            P("dp", "tensor"),
            P("tensor", None),
            P("dp", "tensor"),
            P("dp"),
        ),
        out_specs=(P("dp", "tensor"), P("dp", "tensor"), P("dp", "tensor"), P("dp", "tensor")),
        check_vma=False,
    )
```

```python
import math

import jax
import jax.numpy as jnp
from jax import lax
from jax.experimental import pallas as pl
from jax.experimental.pallas import tpu as pltpu
from jax.sharding import PartitionSpec as P

HEADS = 8
HEAD_SIZE = 128
TOK = 128
PAIR = 2 * TOK
DOCS = 16
ROWS = TOK + DOCS
SLOTS = 9
KEYS = SLOTS * PAIR
STEP = 2 * PAIR
CHUNK = 256
QROWS = HEADS * TOK
FEATURES = 512
MASKED = -1e30
SCALE = 1.0 / math.sqrt(HEAD_SIZE)
SCALE_LOG2 = SCALE * math.log2(math.e)

VMEM = pl.BlockSpec(memory_space=pltpu.VMEM)
SMEM = pl.BlockSpec(memory_space=pltpu.SMEM)
NT = (((1,), (1,)), ((), ()))

PLACE = {0: (0, 0), 4: (0, 1), 8: (1, 0), 1: (2, 0), 5: (2, 1), 2: (3, 0), 6: (3, 1), 3: (4, 0), 7: (4, 1)}
HELD = (2, 1, 2, 2, 2)


def dot_nt(a, b):
    return lax.dot_general(a, b, NT, preferred_element_type=jnp.float32)


def dot(a, b):
    return jnp.dot(a, b, preferred_element_type=jnp.float32)


def params(mib):
    return pltpu.CompilerParams(vmem_limit_bytes=mib * 1024 * 1024)


def cost(flops, nbytes, trans=0):
    return pl.CostEstimate(flops=flops, bytes_accessed=nbytes, transcendentals=trans)


def shaped(*shape, dtype=jnp.bfloat16):
    return jax.ShapeDtypeStruct(shape, dtype)


def pack_kernel(key_ref, value_ref, id_ref, out_ref):
    out_ref[0, 0:TOK, 0:HEAD_SIZE] = key_ref[...]
    out_ref[0, 0:TOK, HEAD_SIZE : 2 * HEAD_SIZE] = value_ref[...]
    number = lax.broadcasted_iota(jnp.int32, (DOCS, TOK), 0)
    below = jnp.where(id_ref[...] < number, 1.0, 0.0)
    count = jnp.sum(below, axis=1, keepdims=True)
    out_ref[0, TOK:ROWS, :] = jnp.broadcast_to(count, (DOCS, 2 * HEAD_SIZE)).astype(jnp.bfloat16)


def bias_of(base, rows, core, query_pair, first_row):
    row = lax.broadcasted_iota(jnp.int32, (rows, TOK), 0)
    column = lax.broadcasted_iota(jnp.int32, (rows, TOK), 1)
    key_pos = base + jnp.where(row < PAIR, row, row - 2 * PAIR)
    query_pos = query_pair * PAIR + core * TOK + column
    allowed = (key_pos >= first_row) & (key_pos <= query_pos)
    bias = jnp.where(allowed, 0.0, MASKED)
    return jnp.concatenate([bias] * (CHUNK // TOK), 1)


def eights(value):
    return value.reshape(value.shape[0] // 8, 8, value.shape[1])


def forward_kernel(info_ref, q_ref, id_ref, *refs):
    own, sib, refs = refs[:5], refs[5:10], refs[10:]
    att_ref, att_t_ref, log_ref, first_ref, rows_ref, key_ref, value_ref = refs[:7]
    score_ref, acc_ref, max_ref, sum_ref = refs[7:]
    query_pair, core = info_ref[0], info_ref[1]
    at_own = pl.multiple_of(core * TOK, TOK)
    at_sib = pl.multiple_of((1 - core) * TOK, TOK)
    below = jnp.zeros((DOCS, TOK), jnp.float32)
    for j in range(SLOTS):
        array, place = PLACE[j]
        valid = jnp.where(query_pair >= j, 1.0, 0.0)
        for held, at in ((own, at_own), (sib, at_sib)):
            ref = held[array]
            key_ref[pl.ds(j * PAIR + at, TOK), :] = ref[place, 0:TOK, 0:HEAD_SIZE]
            value_ref[pl.ds(j * PAIR + at, TOK), :] = ref[place, 0:TOK, HEAD_SIZE : 2 * HEAD_SIZE]
            below = below + valid * ref[place, TOK:ROWS, 0:TOK].astype(jnp.float32)
    for h in range(HEADS):
        rows_ref[h * TOK : (h + 1) * TOK, :] = q_ref[:, h * HEAD_SIZE : (h + 1) * HEAD_SIZE]
    number = lax.broadcasted_iota(jnp.int32, (DOCS, TOK), 0)
    before = jnp.sum(jnp.where(id_ref[...] == number, below, 0.0), axis=0, keepdims=True)
    first_row = before.astype(jnp.int32) + PAIR * jnp.maximum(query_pair - (SLOTS - 1), 0)
    first_ref[...] = first_row
    live = query_pair - jnp.min(first_row) // PAIR + 1
    max_ref[...] = jnp.full(max_ref.shape, MASKED, jnp.float32)
    sum_ref[...] = jnp.zeros(sum_ref.shape, jnp.float32)
    acc_ref[...] = jnp.zeros(acc_ref.shape, jnp.float32)

    def score_rows(start, count, base):
        rows = pl.ds(start, count)
        key = key_ref[rows, :]
        bias = bias_of(base, count, core, query_pair, first_row)
        for n in range(QROWS // CHUNK):
            cols = slice(n * CHUNK, (n + 1) * CHUNK)
            score = dot_nt(key, rows_ref[cols, :]) * SCALE_LOG2 + bias
            score_ref[rows, cols] = score
            max_ref[:, cols] = jnp.maximum(max_ref[:, cols], jnp.max(eights(score), axis=0))

    def mix_rows(start, count):
        rows = pl.ds(start, count)
        value_t = value_ref[rows, :].T
        for n in range(QROWS // CHUNK):
            cols = slice(n * CHUNK, (n + 1) * CHUNK)
            weight = jnp.exp2(score_ref[rows, cols] - log_ref[:, cols])
            sum_ref[:, cols] = sum_ref[:, cols] + jnp.sum(eights(weight), axis=0)
            acc_ref[:, cols] = acc_ref[:, cols] + dot(value_t, weight.astype(jnp.bfloat16))

    def score_step(s, unused):
        score_rows(pl.multiple_of(PAIR + s * STEP, PAIR), STEP, (query_pair - 1 - 2 * s) * PAIR)
        return unused

    def mix_step(s, unused):
        mix_rows(pl.multiple_of(PAIR + s * STEP, PAIR), STEP)
        return unused

    score_rows(0, PAIR, query_pair * PAIR)
    lax.fori_loop(0, live // 2, score_step, 0)
    log_ref[...] = jnp.max(max_ref[...], axis=0, keepdims=True)
    mix_rows(0, PAIR)
    lax.fori_loop(0, live // 2, mix_step, 0)
    total = jnp.sum(sum_ref[...], axis=0, keepdims=True)
    log_ref[...] = log_ref[...] + jnp.log2(total)
    inverse = 1.0 / total
    for h in range(HEADS):
        cols = slice(h * TOK, (h + 1) * TOK)
        mixed = acc_ref[:, cols] * inverse[:, cols]
        att_t_ref[:, cols] = mixed.astype(jnp.bfloat16)
        att_ref[:, h * HEAD_SIZE : (h + 1) * HEAD_SIZE] = mixed.T.astype(jnp.bfloat16)


def backward_kernel(info_ref, rows_ref, key_ref, value_ref, att_t_ref, grad_ref, log_ref, first_ref, *refs):
    dq_ref, own, sib, refs = refs[0], refs[1:6], refs[6:11], refs[11:]
    grad_t_ref, grows_ref, acc_ref, delta_ref, out_ref = refs
    query_pair, core = info_ref[0], info_ref[1]
    at_own = pl.multiple_of(core * TOK, TOK)
    at_sib = pl.multiple_of((1 - core) * TOK, TOK)
    first_row = first_ref[...]
    live = query_pair - jnp.min(first_row) // PAIR + 1
    for h in range(HEADS):
        part = slice(h * TOK, (h + 1) * TOK)
        grad_t = grad_ref[part, :]
        grad_t_ref[:, part] = grad_t
        grows_ref[part, :] = grad_t.T
        product = grad_t.astype(jnp.float32) * att_t_ref[:, part].astype(jnp.float32)
        delta_ref[:, part] = jnp.sum(product, axis=0, keepdims=True)
    acc_ref[...] = jnp.zeros(acc_ref.shape, jnp.float32)
    out_ref[...] = jnp.zeros(out_ref.shape, jnp.bfloat16)

    def grad_rows(start, count, base):
        rows = pl.ds(start, count)
        key = key_ref[rows, :]
        value = value_ref[rows, :]
        key_t = key.T
        bias = bias_of(base, count, core, query_pair, first_row)
        dkey = jnp.zeros((count, HEAD_SIZE), jnp.float32)
        dvalue = jnp.zeros((count, HEAD_SIZE), jnp.float32)
        for n in range(QROWS // CHUNK):
            cols = slice(n * CHUNK, (n + 1) * CHUNK)
            score = dot_nt(key, rows_ref[cols, :]) * SCALE_LOG2 + bias
            prob = jnp.exp2(score - log_ref[:, cols])
            gprob = dot(value, grad_t_ref[:, cols])
            gscore = (prob * (gprob - delta_ref[:, cols])).astype(jnp.bfloat16)
            dvalue = dvalue + dot(prob.astype(jnp.bfloat16), grows_ref[cols, :])
            dkey = dkey + dot(gscore, rows_ref[cols, :])
            acc_ref[:, cols] = acc_ref[:, cols] + dot(key_t, gscore)
        out_ref[rows, 0:HEAD_SIZE] = (dkey * SCALE).astype(jnp.bfloat16)
        out_ref[rows, HEAD_SIZE : 2 * HEAD_SIZE] = dvalue.astype(jnp.bfloat16)

    def grad_step(s, unused):
        grad_rows(pl.multiple_of(PAIR + s * STEP, PAIR), STEP, (query_pair - 1 - 2 * s) * PAIR)
        return unused

    grad_rows(0, PAIR, query_pair * PAIR)
    lax.fori_loop(0, live // 2, grad_step, 0)
    for j in range(SLOTS):
        array, place = PLACE[j]
        own[array][place] = out_ref[pl.ds(j * PAIR + at_own, TOK), :]
        sib[array][place] = out_ref[pl.ds(j * PAIR + at_sib, TOK), :]
    for h in range(HEADS):
        mixed = acc_ref[:, h * TOK : (h + 1) * TOK] * SCALE
        dq_ref[:, h * HEAD_SIZE : (h + 1) * HEAD_SIZE] = mixed.T.astype(jnp.bfloat16)


def columns_of(info_ref, w_ref, ahead):
    at = lax.rem(info_ref[2] + ahead, 8) * FEATURES
    return w_ref[:, pl.ds(pl.multiple_of(at, FEATURES), FEATURES)]


def project_kernel(aheads, info_ref, att_ref, w_ref, *out_refs):
    attended = att_ref[...]
    for n, ahead in enumerate(aheads):
        ref = out_refs[n * len(out_refs) // len(aheads)]
        ref[n % ref.shape[0]] = dot(attended, columns_of(info_ref, w_ref, ahead)).astype(ref.dtype)


def project(aheads, info, attended, out_weight, outs):
    def kernel(*refs):
        project_kernel(aheads, *refs)

    return pl.pallas_call(
        kernel,
        in_specs=[SMEM, VMEM, VMEM],
        out_specs=[VMEM] * len(outs),
        out_shape=outs,
        compiler_params=params(14),
        cost_estimate=cost(2 * len(aheads) * TOK * QROWS * FEATURES, len(aheads) * QROWS * FEATURES * 2),
    )(info, attended, out_weight)


def cotangent(aheads, info, pieces, start, out_weight, dtype):
    def kernel(info_ref, *refs):
        w_ref, out_ref = refs[-2], refs[-1]
        total = None if start is None else refs[len(pieces)][...]
        n = 0
        for ref in refs[: len(pieces)]:
            for j in range(ref.shape[0] // TOK):
                part = dot_nt(columns_of(info_ref, w_ref, aheads[n]), ref[j * TOK : (j + 1) * TOK, :])
                total = part if total is None else total + part
                n = n + 1
        out_ref[...] = total.astype(out_ref.dtype)

    operands = list(pieces) + ([] if start is None else [start]) + [out_weight]
    return pl.pallas_call(
        kernel,
        in_specs=[SMEM] + [VMEM] * len(operands),
        out_specs=VMEM,
        out_shape=shaped(QROWS, TOK, dtype=dtype),
        compiler_params=params(14),
        cost_estimate=cost(2 * len(aheads) * TOK * QROWS * FEATURES, len(aheads) * QROWS * FEATURES * 2),
    )(info, *operands)


def chips_on(value, by):
    return lax.ppermute(value, "dp", [(i, (i + 2 * by) % 32) for i in range(32)])


def across(value):
    return lax.ppermute(value, "dp", [(i, i ^ 1) for i in range(32)])


def along_z(value, by):
    return lax.ppermute(value, "tensor", [(i, (i + by) % 8) for i in range(8)])


def wide(value):
    return value.astype(jnp.float32)


def low(value):
    return value.astype(jnp.bfloat16)


def forward(info, queries, ids, own, sib):
    return pl.pallas_call(
        forward_kernel,
        in_specs=[SMEM] + [VMEM] * 12,
        out_specs=[VMEM] * 7,
        out_shape=[
            shaped(TOK, QROWS),
            shaped(HEAD_SIZE, QROWS),
            shaped(1, QROWS, dtype=jnp.float32),
            shaped(1, TOK, dtype=jnp.int32),
            shaped(QROWS, HEAD_SIZE),
            shaped(KEYS, HEAD_SIZE),
            shaped(KEYS, HEAD_SIZE),
        ],
        scratch_shapes=[
            pltpu.VMEM((KEYS, QROWS), jnp.float32),
            pltpu.VMEM((HEAD_SIZE, QROWS), jnp.float32),
            pltpu.VMEM((8, QROWS), jnp.float32),
            pltpu.VMEM((8, QROWS), jnp.float32),
        ],
        compiler_params=params(24),
        cost_estimate=cost(4 * KEYS * QROWS * HEAD_SIZE, 4 << 20, KEYS * QROWS),
    )(info, queries, ids, *own, *sib)


def backward(info, rows, key, value, att_t, grad, log_total, first_row):
    pieces = [shaped(n, TOK, 2 * HEAD_SIZE) for n in HELD]
    outs = pl.pallas_call(
        backward_kernel,
        in_specs=[SMEM] + [VMEM] * 7,
        out_specs=[VMEM] * 11,
        out_shape=[shaped(TOK, QROWS)] + pieces + pieces,
        scratch_shapes=[
            pltpu.VMEM((HEAD_SIZE, QROWS), jnp.bfloat16),
            pltpu.VMEM((QROWS, HEAD_SIZE), jnp.bfloat16),
            pltpu.VMEM((HEAD_SIZE, QROWS), jnp.float32),
            pltpu.VMEM((1, QROWS), jnp.float32),
            pltpu.VMEM((KEYS, 2 * HEAD_SIZE), jnp.bfloat16),
        ],
        compiler_params=params(20),
        cost_estimate=cost(10 * KEYS * QROWS * HEAD_SIZE, 4 << 20, KEYS * QROWS),
    )(info, rows, key, value, att_t, grad, log_total, first_row)
    return outs[0], outs[1:6], outs[6:11]


def per_device(rotated_queries, rotated_keys, value_heads_packed, out_weight, out_cotangent, doc_ids):
    me = lax.axis_index("dp").astype(jnp.int32)
    z = lax.axis_index("tensor").astype(jnp.int32)
    info = jnp.stack([me // 2, me % 2, z])
    ids = doc_ids.reshape(1, TOK)

    block = pl.pallas_call(
        pack_kernel,
        in_specs=[VMEM] * 3,
        out_specs=VMEM,
        out_shape=shaped(1, ROWS, 2 * HEAD_SIZE),
        compiler_params=params(2),
    )(rotated_keys, value_heads_packed, ids)
    block_4 = chips_on(block, 4)
    block_8 = chips_on(block, 8)
    z_up, z_down, z_four = along_z(out_cotangent, -1), along_z(out_cotangent, 1), along_z(out_cotangent, 4)
    near = jnp.concatenate([block, block_4], 0)
    own = [near, block_8] + [chips_on(near, by) for by in (1, 2, 3)]
    sib = [across(piece) for piece in own]
    z_far_up = along_z(jnp.concatenate([z_up, z_four], 0), -1)
    z_far_down = along_z(jnp.concatenate([z_down, z_four], 0), 1)

    grad_near = cotangent((0, 1, 7, 4), info, [out_cotangent, z_up, z_down, z_four], None, out_weight, jnp.float32)
    grad_t = cotangent((2, 5, 6, 3), info, [z_far_up, z_far_down], grad_near, out_weight, jnp.bfloat16)

    attended, att_t, log_total, first_row, rows, key, value = forward(info, rotated_queries, ids, own, sib)
    to_up, to_down = project((2, 5, 6, 3), info, attended, out_weight, [shaped(2, TOK, FEATURES)] * 2)
    near_up, near_four, near_down, kept = project(
        (1, 4, 7, 0), info, attended, out_weight, [shaped(1, TOK, FEATURES, dtype=jnp.float32)] * 4
    )
    att_t, to_up, to_down, near_up, near_four, near_down, kept = lax.optimization_barrier(
        (att_t, to_up, to_down, near_up, near_four, near_down, kept)
    )
    got_up = along_z(to_up, 1)
    got_down = along_z(to_down, -1)

    query_grad, grad_own, grad_sib = backward(info, rows, key, value, att_t, grad_t, log_total, first_row)

    sum_up = along_z(low(near_up[0] + wide(got_up[0])), 1)
    sum_four = along_z(low(near_four[0] + wide(got_up[1]) + wide(got_down[1])), 4)
    sum_down = along_z(low(near_down[0] + wide(got_down[0])), -1)
    projected = low(kept[0] + wide(sum_up) + wide(sum_four) + wide(sum_down))

    both = [wide(mine) + wide(across(theirs)) for mine, theirs in zip(grad_own, grad_sib)]
    back = [wide(chips_on(low(both[2 + n]), -(n + 1))) for n in range(3)]
    back_8 = wide(chips_on(low(both[1]), -8))
    near_sum = both[0] + back[0] + back[1] + back[2]
    total = near_sum[0] + back_8[0] + wide(chips_on(low(near_sum[1]), -4))
    total = low(total)
    return projected, query_grad, total[:, :HEAD_SIZE], total[:, HEAD_SIZE:]


def solution(mesh):
    return jax.shard_map(
        per_device,
        mesh=mesh,
        in_specs=(
            P("dp", "tensor"),
            P("dp", "tensor"),
            P("dp", "tensor"),
            P("tensor", None),
            P("dp", "tensor"),
            P("dp"),
        ),
        out_specs=(P("dp", "tensor"), P("dp", "tensor"), P("dp", "tensor"), P("dp", "tensor")),
        check_vma=False,
    )
```

```python
import math

import jax
import jax.numpy as jnp
from jax import lax
from jax.experimental import pallas as pl
from jax.experimental.pallas import tpu as pltpu
from jax.sharding import PartitionSpec as P

HEADS = 8
HEAD_SIZE = 128
TOK = 128
PAIR = 2 * TOK
DOCS = 16
ROWS = TOK + DOCS
SLOTS = 9
KEYS = SLOTS * PAIR
STEP = 2 * PAIR
CHUNK = 256
QROWS = HEADS * TOK
FEATURES = 512
MASKED = -1e30
SCALE = 1.0 / math.sqrt(HEAD_SIZE)
SCALE_LOG2 = SCALE * math.log2(math.e)

VMEM = pl.BlockSpec(memory_space=pltpu.VMEM)
SMEM = pl.BlockSpec(memory_space=pltpu.SMEM)
HBM = pl.BlockSpec(memory_space=pltpu.HBM)
NT = (((1,), (1,)), ((), ()))

PLACE = {0: (0, 0), 4: (0, 1), 8: (1, 0), 1: (2, 0), 5: (2, 1), 2: (3, 0), 6: (3, 1), 3: (4, 0), 7: (4, 1)}
HELD = (2, 1, 2, 2, 2)
PROJECT_ORDER = (2, 5, 6, 3, 1, 4, 7, 0)
GRADIENT_ORDER = (0, 1, 7, 4, 2, 5, 6, 3)
WEIGHT_FLOPS = 2 * TOK * QROWS * 8 * FEATURES


def dot_nt(a, b):
    return lax.dot_general(a, b, NT, preferred_element_type=jnp.float32)


def dot(a, b):
    return jnp.dot(a, b, preferred_element_type=jnp.float32)


def params(mib):
    return pltpu.CompilerParams(vmem_limit_bytes=mib * 1024 * 1024)


def cost(flops, nbytes, trans=0):
    return pl.CostEstimate(flops=flops, bytes_accessed=nbytes, transcendentals=trans)


def shaped(*shape, dtype=jnp.bfloat16):
    return jax.ShapeDtypeStruct(shape, dtype)


def pack_kernel(key_ref, value_ref, id_ref, out_ref, ids_ref, sems):
    places = (out_ref.at[0, 0:TOK, 0:HEAD_SIZE], out_ref.at[0, 0:TOK, HEAD_SIZE : 2 * HEAD_SIZE], ids_ref)
    copies = [
        pltpu.make_async_copy(source, place, sems.at[n])
        for n, (source, place) in enumerate(zip((key_ref, value_ref, id_ref), places))
    ]
    for copy in copies:
        copy.start()
    number = lax.broadcasted_iota(jnp.int32, (DOCS, TOK), 0)
    copies[2].wait()
    below = jnp.where(ids_ref[...] < number, 1.0, 0.0)
    count = jnp.sum(below, axis=1, keepdims=True)
    out_ref[0, TOK:ROWS, :] = jnp.broadcast_to(count, (DOCS, 2 * HEAD_SIZE)).astype(jnp.bfloat16)
    copies[0].wait()
    copies[1].wait()


def fetch_weight(aheads, z, w_ref, held_ref, sems):
    copies = []
    for n, ahead in enumerate(aheads):
        at = pl.multiple_of(lax.rem(z + ahead, 8) * FEATURES, FEATURES)
        copies.append(pltpu.make_async_copy(w_ref.at[:, pl.ds(at, FEATURES)], held_ref.at[n], sems.at[n]))
    for copy in copies:
        copy.start()
    return copies


def bias_of(base, rows, core, query_pair, first_row):
    row = lax.broadcasted_iota(jnp.int32, (rows, TOK), 0)
    column = lax.broadcasted_iota(jnp.int32, (rows, TOK), 1)
    key_pos = base + jnp.where(row < PAIR, row, row - 2 * PAIR)
    query_pos = query_pair * PAIR + core * TOK + column
    allowed = (key_pos >= first_row) & (key_pos <= query_pos)
    bias = jnp.where(allowed, 0.0, MASKED)
    return jnp.concatenate([bias] * (CHUNK // TOK), 1)


def eights(value):
    return value.reshape(value.shape[0] // 8, 8, value.shape[1])


def forward_kernel(info_ref, q_ref, w_ref, id_ref, *refs):
    own, sib, refs = refs[:5], refs[5:10], refs[10:]
    att_t_ref, log_ref, first_ref, rows_ref, key_ref, value_ref = refs[:6]
    sends, keeps, refs = refs[6:8], refs[8:12], refs[12:]
    score_ref, acc_ref, max_ref, sum_ref, att_ref, held_ref, sems, q_sems = refs
    query_pair, core = info_ref[0], info_ref[1]
    q_copies = [
        pltpu.make_async_copy(
            q_ref.at[:, pl.ds(h * HEAD_SIZE, HEAD_SIZE)], rows_ref.at[pl.ds(h * TOK, TOK)], q_sems.at[h]
        )
        for h in range(HEADS)
    ]
    for copy in q_copies:
        copy.start()
    w_copies = fetch_weight(PROJECT_ORDER, info_ref[2], w_ref, held_ref, sems)
    at_own = pl.multiple_of(core * TOK, TOK)
    at_sib = pl.multiple_of((1 - core) * TOK, TOK)
    below = jnp.zeros((DOCS, TOK), jnp.float32)
    for j in range(SLOTS):
        array, place = PLACE[j]
        valid = jnp.where(query_pair >= j, 1.0, 0.0)
        for held, at in ((own, at_own), (sib, at_sib)):
            ref = held[array]
            key_ref[pl.ds(j * PAIR + at, TOK), :] = ref[place, 0:TOK, 0:HEAD_SIZE]
            value_ref[pl.ds(j * PAIR + at, TOK), :] = ref[place, 0:TOK, HEAD_SIZE : 2 * HEAD_SIZE]
            below = below + valid * ref[place, TOK:ROWS, 0:TOK].astype(jnp.float32)
    number = lax.broadcasted_iota(jnp.int32, (DOCS, TOK), 0)
    before = jnp.sum(jnp.where(id_ref[...] == number, below, 0.0), axis=0, keepdims=True)
    first_row = before.astype(jnp.int32) + PAIR * jnp.maximum(query_pair - (SLOTS - 1), 0)
    first_ref[...] = first_row
    live = query_pair - jnp.min(first_row) // PAIR + 1
    max_ref[...] = jnp.full(max_ref.shape, MASKED, jnp.float32)
    sum_ref[...] = jnp.zeros(sum_ref.shape, jnp.float32)
    acc_ref[...] = jnp.zeros(acc_ref.shape, jnp.float32)

    def score_rows(start, count, base):
        rows = pl.ds(start, count)
        key = key_ref[rows, :]
        bias = bias_of(base, count, core, query_pair, first_row)
        for n in range(QROWS // CHUNK):
            cols = slice(n * CHUNK, (n + 1) * CHUNK)
            score = dot_nt(key, rows_ref[cols, :]) * SCALE_LOG2 + bias
            score_ref[rows, cols] = score
            max_ref[:, cols] = jnp.maximum(max_ref[:, cols], jnp.max(eights(score), axis=0))

    def mix_rows(start, count):
        rows = pl.ds(start, count)
        value_t = value_ref[rows, :].T
        for n in range(QROWS // CHUNK):
            cols = slice(n * CHUNK, (n + 1) * CHUNK)
            weight = jnp.exp2(score_ref[rows, cols] - log_ref[:, cols])
            sum_ref[:, cols] = sum_ref[:, cols] + jnp.sum(eights(weight), axis=0)
            acc_ref[:, cols] = acc_ref[:, cols] + dot(value_t, weight.astype(jnp.bfloat16))

    def score_step(s, unused):
        score_rows(pl.multiple_of(PAIR + s * STEP, PAIR), STEP, (query_pair - 1 - 2 * s) * PAIR)
        return unused

    def mix_step(s, unused):
        mix_rows(pl.multiple_of(PAIR + s * STEP, PAIR), STEP)
        return unused

    for copy in q_copies:
        copy.wait()
    score_rows(0, PAIR, query_pair * PAIR)
    lax.fori_loop(0, live // 2, score_step, 0)
    log_ref[...] = jnp.max(max_ref[...], axis=0, keepdims=True)
    mix_rows(0, PAIR)
    lax.fori_loop(0, live // 2, mix_step, 0)
    total = jnp.sum(sum_ref[...], axis=0, keepdims=True)
    log_ref[...] = log_ref[...] + jnp.log2(total)
    inverse = 1.0 / total
    for h in range(HEADS):
        cols = slice(h * TOK, (h + 1) * TOK)
        mixed = acc_ref[:, cols] * inverse[:, cols]
        att_t_ref[:, cols] = mixed.astype(jnp.bfloat16)
        att_ref[:, h * HEAD_SIZE : (h + 1) * HEAD_SIZE] = mixed.T.astype(jnp.bfloat16)
    for n in range(8):
        w_copies[n].wait()
        part = dot(att_ref[...], held_ref[n])
        if n < 4:
            sends[n // 2][n % 2] = part.astype(jnp.bfloat16)
        else:
            keeps[n - 4][...] = part


def backward_kernel(info_ref, cot_ref, w_ref, *refs):
    pieces, refs = refs[:5], refs[5:]
    rows_ref, key_ref, value_ref, att_t_ref, log_ref, first_ref = refs[:6]
    dq_ref, own, sib, refs = refs[6], refs[7:12], refs[12:17], refs[17:]
    grad_ref, grad_t_ref, grows_ref, acc_ref, delta_ref, out_ref, mine_ref, held_ref, sems, cot_sem = refs
    query_pair, core = info_ref[0], info_ref[1]
    cot_copy = pltpu.make_async_copy(cot_ref, mine_ref, cot_sem)
    cot_copy.start()
    w_copies = fetch_weight(GRADIENT_ORDER, info_ref[2], w_ref, held_ref, sems)
    at_own = pl.multiple_of(core * TOK, TOK)
    at_sib = pl.multiple_of((1 - core) * TOK, TOK)
    first_row = first_ref[...]
    live = query_pair - jnp.min(first_row) // PAIR + 1
    cot_copy.wait()
    n = 0
    for ref in (mine_ref,) + pieces:
        for j in range(ref.shape[0] // TOK):
            w_copies[n].wait()
            part = dot_nt(held_ref[n], ref[j * TOK : (j + 1) * TOK, :])
            grad_ref[...] = part if n == 0 else grad_ref[...] + part
            n = n + 1
    for h in range(HEADS):
        part = slice(h * TOK, (h + 1) * TOK)
        grad_t = grad_ref[part, :].astype(jnp.bfloat16)
        grad_t_ref[:, part] = grad_t
        grows_ref[part, :] = grad_t.T
        product = grad_t.astype(jnp.float32) * att_t_ref[:, part].astype(jnp.float32)
        delta_ref[:, part] = jnp.sum(product, axis=0, keepdims=True)
    acc_ref[...] = jnp.zeros(acc_ref.shape, jnp.float32)
    out_ref[...] = jnp.zeros(out_ref.shape, jnp.bfloat16)

    def grad_rows(start, count, base):
        rows = pl.ds(start, count)
        key = key_ref[rows, :]
        value = value_ref[rows, :]
        key_t = key.T
        bias = bias_of(base, count, core, query_pair, first_row)
        dkey = jnp.zeros((count, HEAD_SIZE), jnp.float32)
        dvalue = jnp.zeros((count, HEAD_SIZE), jnp.float32)
        for n in range(QROWS // CHUNK):
            cols = slice(n * CHUNK, (n + 1) * CHUNK)
            score = dot_nt(key, rows_ref[cols, :]) * SCALE_LOG2 + bias
            prob = jnp.exp2(score - log_ref[:, cols])
            gprob = dot(value, grad_t_ref[:, cols])
            gscore = (prob * (gprob - delta_ref[:, cols])).astype(jnp.bfloat16)
            dvalue = dvalue + dot(prob.astype(jnp.bfloat16), grows_ref[cols, :])
            dkey = dkey + dot(gscore, rows_ref[cols, :])
            acc_ref[:, cols] = acc_ref[:, cols] + dot(key_t, gscore)
        out_ref[rows, 0:HEAD_SIZE] = (dkey * SCALE).astype(jnp.bfloat16)
        out_ref[rows, HEAD_SIZE : 2 * HEAD_SIZE] = dvalue.astype(jnp.bfloat16)

    def grad_step(s, unused):
        grad_rows(pl.multiple_of(PAIR + s * STEP, PAIR), STEP, (query_pair - 1 - 2 * s) * PAIR)
        return unused

    grad_rows(0, PAIR, query_pair * PAIR)
    lax.fori_loop(0, live // 2, grad_step, 0)
    for j in range(SLOTS):
        array, place = PLACE[j]
        own[array][place] = out_ref[pl.ds(j * PAIR + at_own, TOK), :]
        sib[array][place] = out_ref[pl.ds(j * PAIR + at_sib, TOK), :]
    for h in range(HEADS):
        mixed = acc_ref[:, h * TOK : (h + 1) * TOK] * SCALE
        dq_ref[:, h * HEAD_SIZE : (h + 1) * HEAD_SIZE] = mixed.T.astype(jnp.bfloat16)


def chips_on(value, by):
    return lax.ppermute(value, "dp", [(i, (i + 2 * by) % 32) for i in range(32)])


def across(value):
    return lax.ppermute(value, "dp", [(i, i ^ 1) for i in range(32)])


def along_z(value, by):
    return lax.ppermute(value, "tensor", [(i, (i + by) % 8) for i in range(8)])


def wide(value):
    return value.astype(jnp.float32)


def low(value):
    return value.astype(jnp.bfloat16)


def forward(info, queries, weight, ids, own, sib):
    outs = pl.pallas_call(
        forward_kernel,
        in_specs=[SMEM, HBM, HBM] + [VMEM] * 11,
        out_specs=[VMEM] * 12,
        out_shape=[
            shaped(HEAD_SIZE, QROWS),
            shaped(1, QROWS, dtype=jnp.float32),
            shaped(1, TOK, dtype=jnp.int32),
            shaped(QROWS, HEAD_SIZE),
            shaped(KEYS, HEAD_SIZE),
            shaped(KEYS, HEAD_SIZE),
        ]
        + [shaped(2, TOK, FEATURES)] * 2
        + [shaped(TOK, FEATURES, dtype=jnp.float32)] * 4,
        scratch_shapes=[
            pltpu.VMEM((KEYS, QROWS), jnp.float32),
            pltpu.VMEM((HEAD_SIZE, QROWS), jnp.float32),
            pltpu.VMEM((8, QROWS), jnp.float32),
            pltpu.VMEM((8, QROWS), jnp.float32),
            pltpu.VMEM((TOK, QROWS), jnp.bfloat16),
            pltpu.VMEM((8, QROWS, FEATURES), jnp.bfloat16),
            pltpu.SemaphoreType.DMA((8,)),
            pltpu.SemaphoreType.DMA((HEADS,)),
        ],
        compiler_params=params(46),
        cost_estimate=cost(9_000_000_000, 1 << 20),
    )(info, queries, weight, ids, *own, *sib)
    return outs[:6], outs[6:8], outs[8:]


def backward(info, cotangent, weight, pieces, saved):
    att_t, log_total, first_row, rows, key, value = saved
    blocks = [shaped(n, TOK, 2 * HEAD_SIZE) for n in HELD]
    outs = pl.pallas_call(
        backward_kernel,
        in_specs=[SMEM, HBM, HBM] + [VMEM] * 11,
        out_specs=[VMEM] * 11,
        out_shape=[shaped(TOK, QROWS)] + blocks + blocks,
        scratch_shapes=[
            pltpu.VMEM((QROWS, TOK), jnp.float32),
            pltpu.VMEM((HEAD_SIZE, QROWS), jnp.bfloat16),
            pltpu.VMEM((QROWS, HEAD_SIZE), jnp.bfloat16),
            pltpu.VMEM((HEAD_SIZE, QROWS), jnp.float32),
            pltpu.VMEM((1, QROWS), jnp.float32),
            pltpu.VMEM((KEYS, 2 * HEAD_SIZE), jnp.bfloat16),
            pltpu.VMEM((TOK, FEATURES), jnp.bfloat16),
            pltpu.VMEM((8, QROWS, FEATURES), jnp.bfloat16),
            pltpu.SemaphoreType.DMA((8,)),
            pltpu.SemaphoreType.DMA,
        ],
        compiler_params=params(46),
        cost_estimate=cost(14_000_000_000, 1 << 20),
    )(info, cotangent, weight, *pieces, rows, key, value, att_t, log_total, first_row)
    return outs[0], outs[1:6], outs[6:11]


def per_device(rotated_queries, rotated_keys, value_heads_packed, out_weight, out_cotangent, doc_ids):
    me = lax.axis_index("dp").astype(jnp.int32)
    z = lax.axis_index("tensor").astype(jnp.int32)
    info = jnp.stack([me // 2, me % 2, z])

    block, ids = pl.pallas_call(
        pack_kernel,
        in_specs=[HBM] * 3,
        out_specs=[VMEM] * 2,
        out_shape=[shaped(1, ROWS, 2 * HEAD_SIZE), shaped(1, TOK, dtype=jnp.int32)],
        scratch_shapes=[pltpu.SemaphoreType.DMA((3,))],
        compiler_params=params(2),
        cost_estimate=cost(1_000_000_000, 1 << 16),
    )(rotated_keys, value_heads_packed, doc_ids.reshape(1, TOK))
    block_4 = chips_on(block, 4)
    block_8 = chips_on(block, 8)
    z_up, z_down, z_four = along_z(out_cotangent, -1), along_z(out_cotangent, 1), along_z(out_cotangent, 4)
    near = jnp.concatenate([block, block_4], 0)
    own = [near, block_8] + [chips_on(near, by) for by in (1, 2, 3)]
    sib = [across(piece) for piece in own]
    own, sib, z_up, z_down, z_four = lax.optimization_barrier((own, sib, z_up, z_down, z_four))
    z_far_up = along_z(jnp.concatenate([z_up, z_four], 0), -1)
    z_far_down = along_z(jnp.concatenate([z_down, z_four], 0), 1)

    saved, (to_up, to_down), (near_up, near_four, near_down, kept) = forward(
        info, rotated_queries, out_weight, ids, own, sib
    )
    got_up = along_z(to_up, 1)
    got_down = along_z(to_down, -1)

    pieces = (z_up, z_down, z_four, z_far_up, z_far_down)
    query_grad, grad_own, grad_sib = backward(info, out_cotangent, out_weight, pieces, saved)

    grad_sib, got_up, got_down = lax.optimization_barrier((grad_sib, got_up, got_down))
    sum_up = along_z(low(near_up + wide(got_up[0])), 1)
    sum_four = along_z(low(near_four + wide(got_up[1]) + wide(got_down[1])), 4)
    sum_down = along_z(low(near_down + wide(got_down[0])), -1)
    projected = low(kept + wide(sum_up) + wide(sum_four) + wide(sum_down))

    both = [wide(mine) + wide(across(theirs)) for mine, theirs in zip(grad_own, grad_sib)]
    back = [wide(chips_on(low(both[2 + n]), -(n + 1))) for n in range(3)]
    back_8 = wide(chips_on(low(both[1]), -8))
    near_sum = both[0] + back[0] + back[1] + back[2]
    total = near_sum[0] + back_8[0] + wide(chips_on(low(near_sum[1]), -4))
    total = low(total)
    return projected, query_grad, total[:, :HEAD_SIZE], total[:, HEAD_SIZE:]


def solution(mesh):
    return jax.shard_map(
        per_device,
        mesh=mesh,
        in_specs=(
            P("dp", "tensor"),
            P("dp", "tensor"),
            P("dp", "tensor"),
            P("tensor", None),
            P("dp", "tensor"),
            P("dp"),
        ),
        out_specs=(P("dp", "tensor"), P("dp", "tensor"), P("dp", "tensor"), P("dp", "tensor")),
        check_vma=False,
    )
```

```python
import math

import jax
import jax.numpy as jnp
from jax import lax
from jax.experimental import pallas as pl
from jax.experimental.pallas import tpu as pltpu
from jax.sharding import PartitionSpec as P

HEADS = 8
HEAD_SIZE = 128
TOK = 128
PAIR = 2 * TOK
DOCS = 16
ROWS = TOK + DOCS
SLOTS = 9
KEYS = SLOTS * PAIR
STEP = 2 * PAIR
CHUNK = 256
QROWS = HEADS * TOK
FEATURES = 512
MASKED = -1e30
SCALE = 1.0 / math.sqrt(HEAD_SIZE)
SCALE_LOG2 = SCALE * math.log2(math.e)

VMEM = pl.BlockSpec(memory_space=pltpu.VMEM)
SMEM = pl.BlockSpec(memory_space=pltpu.SMEM)
HBM = pl.BlockSpec(memory_space=pltpu.HBM)
NT = (((1,), (1,)), ((), ()))

PLACE = {0: (0, 0), 4: (0, 1), 8: (1, 0), 1: (2, 0), 5: (2, 1), 2: (3, 0), 6: (3, 1), 3: (4, 0), 7: (4, 1)}
HELD = (2, 1, 2, 2, 2)
PART_ORDER = (2, 5, 6, 3, 1, 4, 7, 0)
FORWARD_MIB = 40
BACKWARD_MIB = 36


def dot_nt(a, b):
    return lax.dot_general(a, b, NT, preferred_element_type=jnp.float32)


def dot(a, b):
    return jnp.dot(a, b, preferred_element_type=jnp.float32)


def params(mib):
    return pltpu.CompilerParams(vmem_limit_bytes=mib * 1024 * 1024)


def cost(flops, nbytes, trans=0):
    return pl.CostEstimate(flops=flops, bytes_accessed=nbytes, transcendentals=trans)


def shaped(*shape, dtype=jnp.bfloat16):
    return jax.ShapeDtypeStruct(shape, dtype)


def packed(keys, values, ids):
    count = jnp.sum(ids[None, :] < jnp.arange(DOCS, dtype=jnp.int32)[:, None], axis=1).astype(jnp.bfloat16)
    counts = jnp.broadcast_to(count[:, None], (DOCS, TOK))
    numbers = jnp.broadcast_to(ids.astype(jnp.bfloat16)[None, :], (DOCS, TOK))
    rows = jnp.concatenate([keys, values], 1)
    return jnp.concatenate([rows, jnp.concatenate([counts, numbers], 1)], 0)[None]


def fetch_weight(aheads, z, w_ref, held_ref, sems):
    copies = []
    for n, ahead in enumerate(aheads):
        at = pl.multiple_of(lax.rem(z + ahead, 8) * FEATURES, FEATURES)
        copies.append(pltpu.make_async_copy(w_ref.at[:, pl.ds(at, FEATURES)], held_ref.at[:, pl.ds(n * FEATURES, FEATURES)], sems.at[n]))
    for copy in copies:
        copy.start()
    return copies


def bias_of(base, rows, core, query_pair, first_row):
    row = lax.broadcasted_iota(jnp.int32, (rows, TOK), 0)
    column = lax.broadcasted_iota(jnp.int32, (rows, TOK), 1)
    key_pos = base + jnp.where(row < PAIR, row, row - 2 * PAIR)
    query_pos = query_pair * PAIR + core * TOK + column
    allowed = (key_pos >= first_row) & (key_pos <= query_pos)
    bias = jnp.where(allowed, 0.0, MASKED)
    return jnp.concatenate([bias] * (CHUNK // TOK), 1)


def eights(value):
    return value.reshape(value.shape[0] // 8, 8, value.shape[1])


def forward_kernel(info_ref, w_ref, rows_ref, *refs):
    own, sib, refs = refs[:5], refs[5:10], refs[10:]
    att_t_ref, log_ref, first_ref, key_ref, value_ref, held_ref = refs[:6]
    sends, keeps, refs = refs[6:8], refs[8:12], refs[12:]
    score_ref, acc_ref, max_ref, sum_ref, att_ref, sems = refs
    query_pair, core = info_ref[0], info_ref[1]
    w_copies = fetch_weight(PART_ORDER, info_ref[2], w_ref, held_ref, sems)
    at_own = pl.multiple_of(core * TOK, TOK)
    at_sib = pl.multiple_of((1 - core) * TOK, TOK)
    below = jnp.zeros((DOCS, TOK), jnp.float32)
    for j in range(SLOTS):
        array, place = PLACE[j]
        valid = jnp.where(query_pair >= j, 1.0, 0.0)
        for held, at in ((own, at_own), (sib, at_sib)):
            ref = held[array]
            key_ref[pl.ds(j * PAIR + at, TOK), :] = ref[place, 0:TOK, 0:HEAD_SIZE]
            value_ref[pl.ds(j * PAIR + at, TOK), :] = ref[place, 0:TOK, HEAD_SIZE : 2 * HEAD_SIZE]
            below = below + valid * ref[place, TOK:ROWS, 0:TOK].astype(jnp.float32)
    number = lax.broadcasted_iota(jnp.int32, (DOCS, TOK), 0)
    numbers = own[0][0, TOK:ROWS, TOK : 2 * TOK].astype(jnp.float32).astype(jnp.int32)
    before = jnp.sum(jnp.where(numbers == number, below, 0.0), axis=0, keepdims=True)
    first_row = before.astype(jnp.int32) + PAIR * jnp.maximum(query_pair - (SLOTS - 1), 0)
    first_ref[...] = first_row
    live = query_pair - jnp.min(first_row) // PAIR + 1
    max_ref[...] = jnp.full(max_ref.shape, MASKED, jnp.float32)
    sum_ref[...] = jnp.zeros(sum_ref.shape, jnp.float32)
    acc_ref[...] = jnp.zeros(acc_ref.shape, jnp.float32)

    def score_rows(start, count, base):
        rows = pl.ds(start, count)
        key = key_ref[rows, :]
        bias = bias_of(base, count, core, query_pair, first_row)
        for n in range(QROWS // CHUNK):
            cols = slice(n * CHUNK, (n + 1) * CHUNK)
            score = dot_nt(key, rows_ref[cols, :]) * SCALE_LOG2 + bias
            score_ref[rows, cols] = score
            max_ref[:, cols] = jnp.maximum(max_ref[:, cols], jnp.max(eights(score), axis=0))

    def mix_rows(start, count):
        rows = pl.ds(start, count)
        value_t = value_ref[rows, :].T
        for n in range(QROWS // CHUNK):
            cols = slice(n * CHUNK, (n + 1) * CHUNK)
            weight = jnp.exp2(score_ref[rows, cols] - log_ref[:, cols])
            sum_ref[:, cols] = sum_ref[:, cols] + jnp.sum(eights(weight), axis=0)
            acc_ref[:, cols] = acc_ref[:, cols] + dot(value_t, weight.astype(jnp.bfloat16))

    def score_step(s, unused):
        score_rows(pl.multiple_of(PAIR + s * STEP, PAIR), STEP, (query_pair - 1 - 2 * s) * PAIR)
        return unused

    def mix_step(s, unused):
        mix_rows(pl.multiple_of(PAIR + s * STEP, PAIR), STEP)
        return unused

    score_rows(0, PAIR, query_pair * PAIR)
    lax.fori_loop(0, live // 2, score_step, 0)
    log_ref[...] = jnp.max(max_ref[...], axis=0, keepdims=True)
    mix_rows(0, PAIR)
    lax.fori_loop(0, live // 2, mix_step, 0)
    total = jnp.sum(sum_ref[...], axis=0, keepdims=True)
    log_ref[...] = log_ref[...] + jnp.log2(total)
    inverse = 1.0 / total
    for h in range(HEADS):
        cols = slice(h * TOK, (h + 1) * TOK)
        mixed = acc_ref[:, cols] * inverse[:, cols]
        att_t_ref[:, cols] = mixed.astype(jnp.bfloat16)
        att_ref[:, h * HEAD_SIZE : (h + 1) * HEAD_SIZE] = mixed.T.astype(jnp.bfloat16)
    for copy in w_copies:
        copy.wait()
    for n in range(8):
        part = dot(att_ref[...], held_ref[:, n * FEATURES : (n + 1) * FEATURES])
        if n < 4:
            sends[n // 2][n % 2] = part.astype(jnp.bfloat16)
        else:
            keeps[n - 4][...] = part


def backward_kernel(info_ref, held_ref, *refs):
    pieces, refs = refs[:6], refs[6:]
    rows_ref, key_ref, value_ref, att_t_ref, log_ref, first_ref = refs[:6]
    dq_ref, own, sib, refs = refs[6], refs[7:12], refs[12:17], refs[17:]
    cot_ref, grad_ref, grad_t_ref, grows_ref, acc_ref, delta_ref, out_ref = refs
    query_pair, core = info_ref[0], info_ref[1]
    at_own = pl.multiple_of(core * TOK, TOK)
    at_sib = pl.multiple_of((1 - core) * TOK, TOK)
    first_row = first_ref[...]
    live = query_pair - jnp.min(first_row) // PAIR + 1
    n = 0
    for ref in pieces:
        for j in range(ref.shape[0] // TOK):
            cot_ref[:, n * FEATURES : (n + 1) * FEATURES] = ref[j * TOK : (j + 1) * TOK, :]
            n = n + 1
    grad_ref[...] = dot_nt(held_ref[...], cot_ref[...])
    for h in range(HEADS):
        part = slice(h * TOK, (h + 1) * TOK)
        grad_t = grad_ref[part, :].astype(jnp.bfloat16)
        grad_t_ref[:, part] = grad_t
        grows_ref[part, :] = grad_t.T
        product = grad_t.astype(jnp.float32) * att_t_ref[:, part].astype(jnp.float32)
        delta_ref[:, part] = jnp.sum(product, axis=0, keepdims=True)
    acc_ref[...] = jnp.zeros(acc_ref.shape, jnp.float32)
    out_ref[...] = jnp.zeros(out_ref.shape, jnp.bfloat16)

    def grad_rows(start, count, base):
        rows = pl.ds(start, count)
        key = key_ref[rows, :]
        value = value_ref[rows, :]
        key_t = key.T
        bias = bias_of(base, count, core, query_pair, first_row)
        dkey = jnp.zeros((count, HEAD_SIZE), jnp.float32)
        dvalue = jnp.zeros((count, HEAD_SIZE), jnp.float32)
        for n in range(QROWS // CHUNK):
            cols = slice(n * CHUNK, (n + 1) * CHUNK)
            score = dot_nt(key, rows_ref[cols, :]) * SCALE_LOG2 + bias
            prob = jnp.exp2(score - log_ref[:, cols])
            gprob = dot(value, grad_t_ref[:, cols])
            gscore = (prob * (gprob - delta_ref[:, cols])).astype(jnp.bfloat16)
            dvalue = dvalue + dot(prob.astype(jnp.bfloat16), grows_ref[cols, :])
            dkey = dkey + dot(gscore, rows_ref[cols, :])
            acc_ref[:, cols] = acc_ref[:, cols] + dot(key_t, gscore)
        out_ref[rows, 0:HEAD_SIZE] = (dkey * SCALE).astype(jnp.bfloat16)
        out_ref[rows, HEAD_SIZE : 2 * HEAD_SIZE] = dvalue.astype(jnp.bfloat16)

    def grad_step(s, unused):
        grad_rows(pl.multiple_of(PAIR + s * STEP, PAIR), STEP, (query_pair - 1 - 2 * s) * PAIR)
        return unused

    grad_rows(0, PAIR, query_pair * PAIR)
    lax.fori_loop(0, live // 2, grad_step, 0)
    for j in range(SLOTS):
        array, place = PLACE[j]
        own[array][place] = out_ref[pl.ds(j * PAIR + at_own, TOK), :]
        sib[array][place] = out_ref[pl.ds(j * PAIR + at_sib, TOK), :]
    for h in range(HEADS):
        mixed = acc_ref[:, h * TOK : (h + 1) * TOK] * SCALE
        dq_ref[:, h * HEAD_SIZE : (h + 1) * HEAD_SIZE] = mixed.T.astype(jnp.bfloat16)


def chips_on(value, by):
    return lax.ppermute(value, "dp", [(i, (i + 2 * by) % 32) for i in range(32)])


def across(value):
    return lax.ppermute(value, "dp", [(i, i ^ 1) for i in range(32)])


def along_z(value, by):
    return lax.ppermute(value, "tensor", [(i, (i + by) % 8) for i in range(8)])


def wide(value):
    return value.astype(jnp.float32)


def low(value):
    return value.astype(jnp.bfloat16)


def forward(info, weight, rows, own, sib):
    outs = pl.pallas_call(
        forward_kernel,
        in_specs=[SMEM, HBM] + [VMEM] * 11,
        out_specs=[VMEM] * 12,
        out_shape=[
            shaped(HEAD_SIZE, QROWS),
            shaped(1, QROWS, dtype=jnp.float32),
            shaped(1, TOK, dtype=jnp.int32),
            shaped(KEYS, HEAD_SIZE),
            shaped(KEYS, HEAD_SIZE),
            shaped(QROWS, 8 * FEATURES),
        ]
        + [shaped(2, TOK, FEATURES)] * 2
        + [shaped(TOK, FEATURES, dtype=jnp.float32)] * 4,
        scratch_shapes=[
            pltpu.VMEM((KEYS, QROWS), jnp.float32),
            pltpu.VMEM((HEAD_SIZE, QROWS), jnp.float32),
            pltpu.VMEM((8, QROWS), jnp.float32),
            pltpu.VMEM((8, QROWS), jnp.float32),
            pltpu.VMEM((TOK, QROWS), jnp.bfloat16),
            pltpu.SemaphoreType.DMA((8,)),
        ],
        compiler_params=params(FORWARD_MIB),
        cost_estimate=cost(9_000_000_000, 1 << 20),
    )(info, weight, rows, *own, *sib)
    return outs[:6], outs[6:8], outs[8:]


def backward(info, pieces, rows, saved):
    att_t, log_total, first_row, key, value, held = saved
    blocks = [shaped(n, TOK, 2 * HEAD_SIZE) for n in HELD]
    outs = pl.pallas_call(
        backward_kernel,
        in_specs=[SMEM] + [VMEM] * 13,
        out_specs=[VMEM] * 11,
        out_shape=[shaped(TOK, QROWS)] + blocks + blocks,
        scratch_shapes=[
            pltpu.VMEM((TOK, 8 * FEATURES), jnp.bfloat16),
            pltpu.VMEM((QROWS, TOK), jnp.float32),
            pltpu.VMEM((HEAD_SIZE, QROWS), jnp.bfloat16),
            pltpu.VMEM((QROWS, HEAD_SIZE), jnp.bfloat16),
            pltpu.VMEM((HEAD_SIZE, QROWS), jnp.float32),
            pltpu.VMEM((1, QROWS), jnp.float32),
            pltpu.VMEM((KEYS, 2 * HEAD_SIZE), jnp.bfloat16),
        ],
        compiler_params=params(BACKWARD_MIB),
        cost_estimate=cost(14_000_000_000, 1 << 20),
    )(info, held, *pieces, rows, key, value, att_t, log_total, first_row)
    return outs[0], outs[1:6], outs[6:11]


def per_device(rotated_queries, rotated_keys, value_heads_packed, out_weight, out_cotangent, doc_ids):
    me = lax.axis_index("dp").astype(jnp.int32)
    z = lax.axis_index("tensor").astype(jnp.int32)
    info = jnp.stack([me // 2, me % 2, z])

    block = packed(rotated_keys, value_heads_packed, doc_ids)
    rows = rotated_queries.reshape(TOK, HEADS, HEAD_SIZE).transpose(1, 0, 2).reshape(QROWS, HEAD_SIZE)
    block_4 = chips_on(block, 4)
    block_8 = chips_on(block, 8)
    z_up, z_down, z_four = along_z(out_cotangent, -1), along_z(out_cotangent, 1), along_z(out_cotangent, 4)
    near = jnp.concatenate([block, block_4], 0)
    near, rows, z_up, z_down, z_four = lax.optimization_barrier((near, rows, z_up, z_down, z_four))
    own = [near, block_8] + [chips_on(near, by) for by in (1, 2, 3)]
    sib = [across(piece) for piece in own]
    z_far_up = along_z(jnp.concatenate([z_up, z_four], 0), -1)
    z_far_down = along_z(jnp.concatenate([z_down, z_four], 0), 1)

    saved, (to_up, to_down), (near_up, near_four, near_down, kept) = forward(
        info, out_weight, rows, own, sib
    )
    got_up = along_z(to_up, 1)
    got_down = along_z(to_down, -1)

    pieces = (z_far_up, z_far_down, z_up, z_four, z_down, out_cotangent)
    query_grad, grad_own, grad_sib = backward(info, pieces, rows, saved)

    grad_sib, got_up, got_down = lax.optimization_barrier((grad_sib, got_up, got_down))
    sum_up = along_z(low(near_up + wide(got_up[0])), 1)
    sum_four = along_z(low(near_four + wide(got_up[1]) + wide(got_down[1])), 4)
    sum_down = along_z(low(near_down + wide(got_down[0])), -1)
    projected = low(kept + wide(sum_up) + wide(sum_four) + wide(sum_down))

    both = [wide(mine) + wide(across(theirs)) for mine, theirs in zip(grad_own, grad_sib)]
    back = [wide(chips_on(low(both[2 + n]), -(n + 1))) for n in range(3)]
    back_8 = wide(chips_on(low(both[1]), -8))
    near_sum = both[0] + back[0] + back[1] + back[2]
    total = near_sum[0] + back_8[0] + wide(chips_on(low(near_sum[1]), -4))
    total = low(total)
    return projected, query_grad, total[:, :HEAD_SIZE], total[:, HEAD_SIZE:]


def solution(mesh):
    return jax.shard_map(
        per_device,
        mesh=mesh,
        in_specs=(
            P("dp", "tensor"),
            P("dp", "tensor"),
            P("dp", "tensor"),
            P("tensor", None),
            P("dp", "tensor"),
            P("dp"),
        ),
        out_specs=(P("dp", "tensor"), P("dp", "tensor"), P("dp", "tensor"), P("dp", "tensor")),
        check_vma=False,
    )
```

```python
import math

import jax
import jax.numpy as jnp
from jax import lax
from jax.experimental import pallas as pl
from jax.experimental.pallas import tpu as pltpu
from jax.sharding import PartitionSpec as P

HEADS = 8
HEAD_SIZE = 128
TOK = 128
PAIR = 2 * TOK
DOCS = 16
ROWS = TOK + DOCS
SLOTS = 9
KEYS = SLOTS * PAIR
STEP = 2 * PAIR
CHUNK = 256
QROWS = HEADS * TOK
FEATURES = 512
MASKED = -1e30
SCALE = 1.0 / math.sqrt(HEAD_SIZE)
SCALE_LOG2 = SCALE * math.log2(math.e)

VMEM = pl.BlockSpec(memory_space=pltpu.VMEM)
SMEM = pl.BlockSpec(memory_space=pltpu.SMEM)
HBM = pl.BlockSpec(memory_space=pltpu.HBM)
NT = (((1,), (1,)), ((), ()))

PLACE = {0: (0, 0), 4: (0, 1), 8: (0, 2), 1: (1, 0), 5: (1, 1), 2: (1, 2), 6: (1, 3), 3: (1, 4), 7: (1, 5)}
HELD = (3, 6)
PART_ORDER = (2, 5, 6, 3, 1, 4, 7, 0)
FORWARD_MIB = 34
BACKWARD_MIB = 12


def dot_nt(a, b):
    return lax.dot_general(a, b, NT, preferred_element_type=jnp.float32)


def dot(a, b):
    return jnp.dot(a, b, preferred_element_type=jnp.float32)


def params(mib):
    return pltpu.CompilerParams(vmem_limit_bytes=mib * 1024 * 1024)


def cost(flops, nbytes, trans=0):
    return pl.CostEstimate(flops=flops, bytes_accessed=nbytes, transcendentals=trans)


def shaped(*shape, dtype=jnp.bfloat16):
    return jax.ShapeDtypeStruct(shape, dtype)


def packed(keys, values, ids):
    numbers = jnp.broadcast_to(jnp.tile(ids, 2).astype(jnp.bfloat16)[None, :], (DOCS, 2 * TOK))
    return jnp.concatenate([jnp.concatenate([keys, values], 1), numbers], 0)[None]


def fetch_weight(aheads, z, w_ref, held_ref, sems):
    copies = []
    for n, ahead in enumerate(aheads):
        at = pl.multiple_of(lax.rem(z + ahead, 8) * FEATURES, FEATURES)
        copies.append(pltpu.make_async_copy(w_ref.at[:, pl.ds(at, FEATURES)], held_ref.at[:, pl.ds(n * FEATURES, FEATURES)], sems.at[n]))
    for copy in copies:
        copy.start()
    return copies


def bias_of(base, rows, core, query_pair, first_row):
    row = lax.broadcasted_iota(jnp.int32, (rows, TOK), 0)
    column = lax.broadcasted_iota(jnp.int32, (rows, TOK), 1)
    key_pos = base + jnp.where(row < PAIR, row, row - 2 * PAIR)
    query_pos = query_pair * PAIR + core * TOK + column
    allowed = (key_pos >= first_row) & (key_pos <= query_pos)
    bias = jnp.where(allowed, 0.0, MASKED)
    return jnp.concatenate([bias] * (CHUNK // TOK), 1)


def eights(value):
    return value.reshape(value.shape[0] // 8, 8, value.shape[1])


def forward_kernel(info_ref, w_ref, rows_ref, *refs):
    own, sib, refs = refs[:2], refs[2:4], refs[4:]
    att_t_ref, inverse_ref, first_ref, key_ref, value_ref, weight_ref, held_ref = refs[:7]
    sends, keeps, refs = refs[7:9], refs[9:13], refs[13:]
    score_ref, acc_ref, max_ref, sum_ref, att_ref, peak_ref, sems = refs
    query_pair, core = info_ref[0], info_ref[1]
    w_copies = fetch_weight(PART_ORDER, info_ref[2], w_ref, held_ref, sems)
    at_own = pl.multiple_of(core * TOK, TOK)
    at_sib = pl.multiple_of((1 - core) * TOK, TOK)
    number = lax.broadcasted_iota(jnp.int32, (DOCS, TOK), 0).astype(jnp.float32)
    below = jnp.zeros((DOCS, TOK), jnp.float32)
    for j in range(SLOTS):
        array, place = PLACE[j]
        valid = jnp.where(query_pair >= j, 1.0, 0.0)
        for held, at in ((own, at_own), (sib, at_sib)):
            ref = held[array]
            key_ref[pl.ds(j * PAIR + at, TOK), :] = ref[place, 0:TOK, 0:HEAD_SIZE]
            value_ref[pl.ds(j * PAIR + at, TOK), :] = ref[place, 0:TOK, HEAD_SIZE : 2 * HEAD_SIZE]
            ids = ref[place, TOK:ROWS, 0:TOK].astype(jnp.float32)
            below = below + jnp.where(ids < number, valid, 0.0)
    below = jnp.sum(below, axis=1, keepdims=True)
    mine = own[0][0, TOK:ROWS, 0:TOK].astype(jnp.float32)
    before = jnp.sum(jnp.where(mine == number, below, 0.0), axis=0, keepdims=True)
    first_row = before.astype(jnp.int32) + PAIR * jnp.maximum(query_pair - (SLOTS - 1), 0)
    first_ref[...] = first_row
    live = query_pair - jnp.min(first_row) // PAIR + 1
    max_ref[...] = jnp.full(max_ref.shape, MASKED, jnp.float32)
    sum_ref[...] = jnp.zeros(sum_ref.shape, jnp.float32)
    acc_ref[...] = jnp.zeros(acc_ref.shape, jnp.float32)

    def score_rows(start, count, base):
        rows = pl.ds(start, count)
        key = key_ref[rows, :]
        bias = bias_of(base, count, core, query_pair, first_row)
        for n in range(QROWS // CHUNK):
            cols = slice(n * CHUNK, (n + 1) * CHUNK)
            score = dot_nt(key, rows_ref[cols, :]) * SCALE_LOG2 + bias
            score_ref[rows, cols] = score
            max_ref[:, cols] = jnp.maximum(max_ref[:, cols], jnp.max(eights(score), axis=0))

    def mix_rows(start, count):
        rows = pl.ds(start, count)
        value_t = value_ref[rows, :].T
        for n in range(QROWS // CHUNK):
            cols = slice(n * CHUNK, (n + 1) * CHUNK)
            weight = jnp.exp2(score_ref[rows, cols] - peak_ref[:, cols])
            sum_ref[:, cols] = sum_ref[:, cols] + jnp.sum(eights(weight), axis=0)
            weight = weight.astype(jnp.bfloat16)
            weight_ref[rows, cols] = weight
            acc_ref[:, cols] = acc_ref[:, cols] + dot(value_t, weight)

    def score_step(s, unused):
        score_rows(pl.multiple_of(PAIR + s * STEP, PAIR), STEP, (query_pair - 1 - 2 * s) * PAIR)
        return unused

    def mix_step(s, unused):
        mix_rows(pl.multiple_of(PAIR + s * STEP, PAIR), STEP)
        return unused

    score_rows(0, PAIR, query_pair * PAIR)
    lax.fori_loop(0, live // 2, score_step, 0)
    peak_ref[...] = jnp.max(max_ref[...], axis=0, keepdims=True)
    mix_rows(0, PAIR)
    lax.fori_loop(0, live // 2, mix_step, 0)
    inverse = 1.0 / jnp.sum(sum_ref[...], axis=0, keepdims=True)
    inverse_ref[...] = inverse
    for h in range(HEADS):
        cols = slice(h * TOK, (h + 1) * TOK)
        mixed = acc_ref[:, cols] * inverse[:, cols]
        att_t_ref[:, cols] = mixed.astype(jnp.bfloat16)
        att_ref[:, h * HEAD_SIZE : (h + 1) * HEAD_SIZE] = mixed.T.astype(jnp.bfloat16)
    for copy in w_copies:
        copy.wait()
    for n in range(8):
        part = dot(att_ref[...], held_ref[:, n * FEATURES : (n + 1) * FEATURES])
        if n < 4:
            sends[n // 2][n % 2] = part.astype(jnp.bfloat16)
        else:
            keeps[n - 4][...] = part


def backward_kernel(info_ref, held_ref, *refs):
    pieces, refs = refs[:6], refs[6:]
    rows_ref, key_ref, value_ref, weight_ref, att_t_ref, inverse_ref, first_ref = refs[:7]
    dq_ref, own, sib, refs = refs[7], refs[8:10], refs[10:12], refs[12:]
    cot_ref, grad_ref, grad_t_ref, grows_ref, acc_ref, delta_ref, out_ref = refs
    query_pair, core = info_ref[0], info_ref[1]
    at_own = pl.multiple_of(core * TOK, TOK)
    at_sib = pl.multiple_of((1 - core) * TOK, TOK)
    live = query_pair - jnp.min(first_ref[...]) // PAIR + 1
    n = 0
    for ref in pieces:
        for j in range(ref.shape[0] // TOK):
            cot_ref[:, n * FEATURES : (n + 1) * FEATURES] = ref[j * TOK : (j + 1) * TOK, :]
            n = n + 1
    grad_ref[...] = dot_nt(held_ref[...], cot_ref[...])
    for h in range(HEADS):
        part = slice(h * TOK, (h + 1) * TOK)
        grad_t = grad_ref[part, :] * inverse_ref[:, part]
        delta_ref[:, part] = jnp.sum(grad_t * att_t_ref[:, part].astype(jnp.float32), axis=0, keepdims=True)
        grad_t = grad_t.astype(jnp.bfloat16)
        grad_t_ref[:, part] = grad_t
        grows_ref[part, :] = grad_t.T
    acc_ref[...] = jnp.zeros(acc_ref.shape, jnp.float32)
    out_ref[...] = jnp.zeros(out_ref.shape, jnp.bfloat16)

    def grad_rows(start, count):
        rows = pl.ds(start, count)
        key_t = key_ref[rows, :].T
        value = value_ref[rows, :]
        dkey = jnp.zeros((count, HEAD_SIZE), jnp.float32)
        dvalue = jnp.zeros((count, HEAD_SIZE), jnp.float32)
        for n in range(QROWS // CHUNK):
            cols = slice(n * CHUNK, (n + 1) * CHUNK)
            weight = weight_ref[rows, cols]
            gprob = dot(value, grad_t_ref[:, cols])
            gscore = (weight.astype(jnp.float32) * (gprob - delta_ref[:, cols])).astype(jnp.bfloat16)
            dvalue = dvalue + dot(weight, grows_ref[cols, :])
            dkey = dkey + dot(gscore, rows_ref[cols, :])
            acc_ref[:, cols] = acc_ref[:, cols] + dot(key_t, gscore)
        out_ref[rows, 0:HEAD_SIZE] = (dkey * SCALE).astype(jnp.bfloat16)
        out_ref[rows, HEAD_SIZE : 2 * HEAD_SIZE] = dvalue.astype(jnp.bfloat16)

    def grad_step(s, unused):
        grad_rows(pl.multiple_of(PAIR + s * STEP, PAIR), STEP)
        return unused

    grad_rows(0, PAIR)
    lax.fori_loop(0, live // 2, grad_step, 0)
    for j in range(SLOTS):
        array, place = PLACE[j]
        own[array][place] = out_ref[pl.ds(j * PAIR + at_own, TOK), :]
        sib[array][place] = out_ref[pl.ds(j * PAIR + at_sib, TOK), :]
    for h in range(HEADS):
        mixed = acc_ref[:, h * TOK : (h + 1) * TOK] * SCALE
        dq_ref[:, h * HEAD_SIZE : (h + 1) * HEAD_SIZE] = mixed.T.astype(jnp.bfloat16)


def chips_on(value, by):
    return lax.ppermute(value, "dp", [(i, (i + 2 * by) % 32) for i in range(32)])


def across(value):
    return lax.ppermute(value, "dp", [(i, i ^ 1) for i in range(32)])


def along_z(value, by):
    return lax.ppermute(value, "tensor", [(i, (i + by) % 8) for i in range(8)])


def wide(value):
    return value.astype(jnp.float32)


def low(value):
    return value.astype(jnp.bfloat16)


def forward(info, weight, rows, own, sib):
    outs = pl.pallas_call(
        forward_kernel,
        in_specs=[SMEM, HBM] + [VMEM] * 5,
        out_specs=[VMEM] * 13,
        out_shape=[
            shaped(HEAD_SIZE, QROWS),
            shaped(1, QROWS, dtype=jnp.float32),
            shaped(1, TOK, dtype=jnp.int32),
            shaped(KEYS, HEAD_SIZE),
            shaped(KEYS, HEAD_SIZE),
            shaped(KEYS, QROWS),
            shaped(QROWS, 8 * FEATURES),
        ]
        + [shaped(2, TOK, FEATURES)] * 2
        + [shaped(TOK, FEATURES, dtype=jnp.float32)] * 4,
        scratch_shapes=[
            pltpu.VMEM((KEYS, QROWS), jnp.float32),
            pltpu.VMEM((HEAD_SIZE, QROWS), jnp.float32),
            pltpu.VMEM((8, QROWS), jnp.float32),
            pltpu.VMEM((8, QROWS), jnp.float32),
            pltpu.VMEM((TOK, QROWS), jnp.bfloat16),
            pltpu.VMEM((1, QROWS), jnp.float32),
            pltpu.SemaphoreType.DMA((8,)),
        ],
        compiler_params=params(FORWARD_MIB),
        cost_estimate=cost(9_000_000_000, 1 << 20),
    )(info, weight, rows, *own, *sib)
    return outs[:7], outs[7:9], outs[9:]


def backward(info, pieces, rows, saved):
    att_t, inverse, first_row, key, value, weight, held = saved
    blocks = [shaped(n, TOK, 2 * HEAD_SIZE) for n in HELD]
    outs = pl.pallas_call(
        backward_kernel,
        in_specs=[SMEM] + [VMEM] * 14,
        out_specs=[VMEM] * 5,
        out_shape=[shaped(TOK, QROWS)] + blocks + blocks,
        scratch_shapes=[
            pltpu.VMEM((TOK, 8 * FEATURES), jnp.bfloat16),
            pltpu.VMEM((QROWS, TOK), jnp.float32),
            pltpu.VMEM((HEAD_SIZE, QROWS), jnp.bfloat16),
            pltpu.VMEM((QROWS, HEAD_SIZE), jnp.bfloat16),
            pltpu.VMEM((HEAD_SIZE, QROWS), jnp.float32),
            pltpu.VMEM((1, QROWS), jnp.float32),
            pltpu.VMEM((KEYS, 2 * HEAD_SIZE), jnp.bfloat16),
        ],
        compiler_params=params(BACKWARD_MIB),
        cost_estimate=cost(14_000_000_000, 1 << 20),
    )(info, held, *pieces, rows, key, value, weight, att_t, inverse, first_row)
    return outs[0], outs[1:3], outs[3:5]


def per_device(rotated_queries, rotated_keys, value_heads_packed, out_weight, out_cotangent, doc_ids):
    me = lax.axis_index("dp").astype(jnp.int32)
    z = lax.axis_index("tensor").astype(jnp.int32)
    info = jnp.stack([me // 2, me % 2, z])

    block = packed(rotated_keys, value_heads_packed, doc_ids)
    rows = rotated_queries.reshape(TOK, HEADS, HEAD_SIZE).transpose(1, 0, 2).reshape(QROWS, HEAD_SIZE)
    block_4 = chips_on(block, 4)
    block_8 = chips_on(block, 8)
    z_up, z_down, z_four = along_z(out_cotangent, -1), along_z(out_cotangent, 1), along_z(out_cotangent, 4)
    near = jnp.concatenate([block, block_4], 0)
    near, rows, z_up, z_down, z_four = lax.optimization_barrier((near, rows, z_up, z_down, z_four))
    own = [
        jnp.concatenate([near, block_8], 0),
        jnp.concatenate([chips_on(near, by) for by in (1, 2, 3)], 0),
    ]
    sib = [across(piece) for piece in own]
    z_far_up = along_z(jnp.concatenate([z_up, z_four], 0), -1)
    z_far_down = along_z(jnp.concatenate([z_down, z_four], 0), 1)

    saved, (to_up, to_down), (near_up, near_four, near_down, kept) = forward(
        info, out_weight, rows, own, sib
    )
    got_up = along_z(to_up, 1)
    got_down = along_z(to_down, -1)

    pieces = (z_far_up, z_far_down, z_up, z_four, z_down, out_cotangent)
    query_grad, grad_own, grad_sib = backward(info, pieces, rows, saved)

    grad_sib, got_up, got_down = lax.optimization_barrier((grad_sib, got_up, got_down))
    sum_up = along_z(low(near_up + wide(got_up[0])), 1)
    sum_four = along_z(low(near_four + wide(got_up[1]) + wide(got_down[1])), 4)
    sum_down = along_z(low(near_down + wide(got_down[0])), -1)
    projected = low(kept + wide(sum_up) + wide(sum_four) + wide(sum_down))

    both = [wide(mine) + wide(across(theirs)) for mine, theirs in zip(grad_own, grad_sib)]
    back = [wide(chips_on(low(both[1][2 * n : 2 * n + 2]), -(n + 1))) for n in range(3)]
    back_8 = wide(chips_on(low(both[0][2]), -8))
    near_sum = both[0][0:2] + back[0] + back[1] + back[2]
    total = near_sum[0] + back_8 + wide(chips_on(low(near_sum[1]), -4))
    total = low(total)
    return projected, query_grad, total[:, :HEAD_SIZE], total[:, HEAD_SIZE:]


def solution(mesh):
    return jax.shard_map(
        per_device,
        mesh=mesh,
        in_specs=(
            P("dp", "tensor"),
            P("dp", "tensor"),
            P("dp", "tensor"),
            P("tensor", None),
            P("dp", "tensor"),
            P("dp"),
        ),
        out_specs=(P("dp", "tensor"), P("dp", "tensor"), P("dp", "tensor"), P("dp", "tensor")),
        check_vma=False,
    )
```

```python
import math

import jax
import jax.numpy as jnp
from jax import lax
from jax.experimental import pallas as pl
from jax.experimental.pallas import tpu as pltpu
from jax.sharding import PartitionSpec as P

HEADS = 8
HEAD_SIZE = 128
TOK = 128
PAIR = 2 * TOK
DOCS = 16
ROWS = TOK + DOCS
SLOTS = 9
KEYS = SLOTS * PAIR
STEP = 2 * PAIR
CHUNK = 256
QROWS = HEADS * TOK
FEATURES = 512
MASKED = -1e30
SCALE = 1.0 / math.sqrt(HEAD_SIZE)
SCALE_LOG2 = SCALE * math.log2(math.e)

VMEM = pl.BlockSpec(memory_space=pltpu.VMEM)
SMEM = pl.BlockSpec(memory_space=pltpu.SMEM)
HBM = pl.BlockSpec(memory_space=pltpu.HBM)
NT = (((1,), (1,)), ((), ()))

PLACE = {0: (0, 0), 4: (0, 1), 8: (0, 2), 1: (1, 0), 5: (1, 1), 2: (1, 2), 6: (1, 3), 3: (1, 4), 7: (1, 5)}
HELD = (3, 6)
PART_ORDER = (2, 5, 6, 3, 1, 4, 7, 0)
FORWARD_MIB = 34
BACKWARD_MIB = 12


def dot_nt(a, b):
    return lax.dot_general(a, b, NT, preferred_element_type=jnp.float32)


def dot(a, b):
    return jnp.dot(a, b, preferred_element_type=jnp.float32)


def params(mib):
    return pltpu.CompilerParams(vmem_limit_bytes=mib * 1024 * 1024)


def cost(flops, nbytes, trans=0):
    return pl.CostEstimate(flops=flops, bytes_accessed=nbytes, transcendentals=trans)


def shaped(*shape, dtype=jnp.bfloat16):
    return jax.ShapeDtypeStruct(shape, dtype)


def packed(keys, values, ids):
    numbers = jnp.broadcast_to(jnp.tile(ids, 2).astype(jnp.bfloat16)[None, :], (DOCS, 2 * TOK))
    return jnp.concatenate([jnp.concatenate([keys, values], 1), numbers], 0)[None]


def fetch_weight(aheads, z, w_ref, held_ref, sems):
    copies = []
    for n, ahead in enumerate(aheads):
        at = pl.multiple_of(lax.rem(z + ahead, 8) * FEATURES, FEATURES)
        copies.append(pltpu.make_async_copy(w_ref.at[:, pl.ds(at, FEATURES)], held_ref.at[:, pl.ds(n * FEATURES, FEATURES)], sems.at[n]))
    for copy in copies:
        copy.start()
    return copies


def bias_of(base, rows, core, query_pair, first_row):
    row = lax.broadcasted_iota(jnp.int32, (rows, TOK), 0)
    column = lax.broadcasted_iota(jnp.int32, (rows, TOK), 1)
    key_pos = base + jnp.where(row < PAIR, row, row - 2 * PAIR)
    query_pos = query_pair * PAIR + core * TOK + column
    allowed = (key_pos >= first_row) & (key_pos <= query_pos)
    bias = jnp.where(allowed, 0.0, MASKED)
    return jnp.concatenate([bias] * (CHUNK // TOK), 1)


def eights(value):
    return value.reshape(value.shape[0] // 8, 8, value.shape[1])


def forward_kernel(info_ref, w_ref, rows_ref, *refs):
    own, sib, refs = refs[:2], refs[2:4], refs[4:]
    att_t_ref, inverse_ref, first_ref, key_ref, value_ref, weight_ref, held_ref = refs[:7]
    sends, keeps, refs = refs[7:9], refs[9:13], refs[13:]
    score_ref, acc_ref, max_ref, sum_ref, att_ref, peak_ref, sems = refs
    query_pair, core = info_ref[0], info_ref[1]
    w_copies = fetch_weight(PART_ORDER, info_ref[2], w_ref, held_ref, sems)
    at_own = pl.multiple_of(core * TOK, TOK)
    at_sib = pl.multiple_of((1 - core) * TOK, TOK)
    number = lax.broadcasted_iota(jnp.int32, (DOCS, TOK), 0).astype(jnp.float32)
    below = jnp.zeros((DOCS, TOK), jnp.float32)
    for j in range(SLOTS):
        array, place = PLACE[j]
        valid = jnp.where(query_pair >= j, 1.0, 0.0)
        for held, at in ((own, at_own), (sib, at_sib)):
            ref = held[array]
            key_ref[pl.ds(j * PAIR + at, TOK), :] = ref[place, 0:TOK, 0:HEAD_SIZE]
            value_ref[pl.ds(j * PAIR + at, TOK), :] = ref[place, 0:TOK, HEAD_SIZE : 2 * HEAD_SIZE]
            ids = ref[place, TOK:ROWS, 0:TOK].astype(jnp.float32)
            below = below + jnp.where(ids < number, valid, 0.0)
    below = jnp.sum(below, axis=1, keepdims=True)
    mine = own[0][0, TOK:ROWS, 0:TOK].astype(jnp.float32)
    before = jnp.sum(jnp.where(mine == number, below, 0.0), axis=0, keepdims=True)
    first_row = before.astype(jnp.int32) + PAIR * jnp.maximum(query_pair - (SLOTS - 1), 0)
    first_ref[...] = first_row
    live = query_pair - jnp.min(first_row) // PAIR + 1
    max_ref[...] = jnp.full(max_ref.shape, MASKED, jnp.float32)
    sum_ref[...] = jnp.zeros(sum_ref.shape, jnp.float32)
    acc_ref[...] = jnp.zeros(acc_ref.shape, jnp.float32)

    def score_rows(start, count, base):
        rows = pl.ds(start, count)
        key = key_ref[rows, :]
        bias = bias_of(base, count, core, query_pair, first_row)
        for n in range(QROWS // CHUNK):
            cols = slice(n * CHUNK, (n + 1) * CHUNK)
            score = dot_nt(key, rows_ref[cols, :]) * SCALE_LOG2 + bias
            score_ref[rows, cols] = score
            max_ref[:, cols] = jnp.maximum(max_ref[:, cols], jnp.max(eights(score), axis=0))

    def mix_rows(start, count):
        rows = pl.ds(start, count)
        value_t = value_ref[rows, :].T
        for n in range(QROWS // CHUNK):
            cols = slice(n * CHUNK, (n + 1) * CHUNK)
            weight = jnp.exp2(score_ref[rows, cols] - peak_ref[:, cols])
            sum_ref[:, cols] = sum_ref[:, cols] + jnp.sum(eights(weight), axis=0)
            weight = weight.astype(jnp.bfloat16)
            weight_ref[rows, cols] = weight
            acc_ref[:, cols] = acc_ref[:, cols] + dot(value_t, weight)

    def score_step(s, unused):
        score_rows(pl.multiple_of(PAIR + s * STEP, PAIR), STEP, (query_pair - 1 - 2 * s) * PAIR)
        return unused

    def mix_step(s, unused):
        mix_rows(pl.multiple_of(PAIR + s * STEP, PAIR), STEP)
        return unused

    score_rows(0, PAIR, query_pair * PAIR)
    lax.fori_loop(0, live // 2, score_step, 0)
    peak_ref[...] = jnp.max(max_ref[...], axis=0, keepdims=True)
    mix_rows(0, PAIR)
    lax.fori_loop(0, live // 2, mix_step, 0)
    inverse = 1.0 / jnp.sum(sum_ref[...], axis=0, keepdims=True)
    inverse_ref[...] = inverse
    for h in range(HEADS):
        cols = slice(h * TOK, (h + 1) * TOK)
        mixed = acc_ref[:, cols] * inverse[:, cols]
        att_t_ref[:, cols] = mixed.astype(jnp.bfloat16)
        att_ref[:, h * HEAD_SIZE : (h + 1) * HEAD_SIZE] = mixed.T.astype(jnp.bfloat16)
    for copy in w_copies:
        copy.wait()
    for n in range(8):
        part = dot(att_ref[...], held_ref[:, n * FEATURES : (n + 1) * FEATURES])
        if n < 4:
            sends[n // 2][n % 2] = part.astype(jnp.bfloat16)
        else:
            keeps[n - 4][...] = part


def backward_kernel(info_ref, held_ref, *refs):
    pieces, refs = refs[:6], refs[6:]
    rows_ref, key_ref, value_ref, weight_ref, att_t_ref, inverse_ref, first_ref = refs[:7]
    dq_ref, own, sib, refs = refs[7], refs[8:10], refs[10:12], refs[12:]
    cot_ref, grad_ref, grad_t_ref, grows_ref, acc_ref, delta_ref, out_ref = refs
    query_pair, core = info_ref[0], info_ref[1]
    at_own = pl.multiple_of(core * TOK, TOK)
    at_sib = pl.multiple_of((1 - core) * TOK, TOK)
    live = query_pair - jnp.min(first_ref[...]) // PAIR + 1
    n = 0
    for ref in pieces:
        for j in range(ref.shape[0] // TOK):
            cot_ref[:, n * FEATURES : (n + 1) * FEATURES] = ref[j * TOK : (j + 1) * TOK, :]
            n = n + 1
    grad_ref[...] = dot_nt(held_ref[...], cot_ref[...])
    for h in range(HEADS):
        part = slice(h * TOK, (h + 1) * TOK)
        grad_t = grad_ref[part, :] * inverse_ref[:, part]
        delta_ref[:, part] = jnp.sum(grad_t * att_t_ref[:, part].astype(jnp.float32), axis=0, keepdims=True)
        grad_t = grad_t.astype(jnp.bfloat16)
        grad_t_ref[:, part] = grad_t
        grows_ref[part, :] = grad_t.T
    acc_ref[...] = jnp.zeros(acc_ref.shape, jnp.float32)
    out_ref[...] = jnp.zeros(out_ref.shape, jnp.bfloat16)

    def grad_rows(start, count):
        rows = pl.ds(start, count)
        key_t = key_ref[rows, :].T
        value = value_ref[rows, :]
        dkey = jnp.zeros((count, HEAD_SIZE), jnp.float32)
        dvalue = jnp.zeros((count, HEAD_SIZE), jnp.float32)
        for n in range(QROWS // CHUNK):
            cols = slice(n * CHUNK, (n + 1) * CHUNK)
            weight = weight_ref[rows, cols]
            gprob = dot(value, grad_t_ref[:, cols])
            gscore = (weight.astype(jnp.float32) * (gprob - delta_ref[:, cols])).astype(jnp.bfloat16)
            dvalue = dvalue + dot(weight, grows_ref[cols, :])
            dkey = dkey + dot(gscore, rows_ref[cols, :])
            acc_ref[:, cols] = acc_ref[:, cols] + dot(key_t, gscore)
        out_ref[rows, 0:HEAD_SIZE] = (dkey * SCALE).astype(jnp.bfloat16)
        out_ref[rows, HEAD_SIZE : 2 * HEAD_SIZE] = dvalue.astype(jnp.bfloat16)

    def grad_step(s, unused):
        grad_rows(pl.multiple_of(PAIR + s * STEP, PAIR), STEP)
        return unused

    grad_rows(0, PAIR)
    lax.fori_loop(0, live // 2, grad_step, 0)
    for j in range(SLOTS):
        array, place = PLACE[j]
        own[array][place] = out_ref[pl.ds(j * PAIR + at_own, TOK), :]
        sib[array][place] = out_ref[pl.ds(j * PAIR + at_sib, TOK), :]
    for h in range(HEADS):
        mixed = acc_ref[:, h * TOK : (h + 1) * TOK] * SCALE
        dq_ref[:, h * HEAD_SIZE : (h + 1) * HEAD_SIZE] = mixed.T.astype(jnp.bfloat16)


def chips_on(value, by):
    return lax.ppermute(value, "dp", [(i, (i + 2 * by) % 32) for i in range(32)])


def across(value):
    return lax.ppermute(value, "dp", [(i, i ^ 1) for i in range(32)])


def along_z(value, by):
    return lax.ppermute(value, "tensor", [(i, (i + by) % 8) for i in range(8)])


def wide(value):
    return value.astype(jnp.float32)


def low(value):
    return value.astype(jnp.bfloat16)


def forward(info, weight, rows, own, sib):
    outs = pl.pallas_call(
        forward_kernel,
        in_specs=[SMEM, HBM] + [VMEM] * 5,
        out_specs=[VMEM] * 13,
        out_shape=[
            shaped(HEAD_SIZE, QROWS),
            shaped(1, QROWS, dtype=jnp.float32),
            shaped(1, TOK, dtype=jnp.int32),
            shaped(KEYS, HEAD_SIZE),
            shaped(KEYS, HEAD_SIZE),
            shaped(KEYS, QROWS),
            shaped(QROWS, 8 * FEATURES),
        ]
        + [shaped(2, TOK, FEATURES)] * 2
        + [shaped(TOK, FEATURES, dtype=jnp.float32)] * 4,
        scratch_shapes=[
            pltpu.VMEM((KEYS, QROWS), jnp.float32),
            pltpu.VMEM((HEAD_SIZE, QROWS), jnp.float32),
            pltpu.VMEM((8, QROWS), jnp.float32),
            pltpu.VMEM((8, QROWS), jnp.float32),
            pltpu.VMEM((TOK, QROWS), jnp.bfloat16),
            pltpu.VMEM((1, QROWS), jnp.float32),
            pltpu.SemaphoreType.DMA((8,)),
        ],
        compiler_params=params(FORWARD_MIB),
        cost_estimate=cost(9_000_000_000, 1 << 20),
    )(info, weight, rows, *own, *sib)
    return outs[:7], outs[7:9], outs[9:]


def backward(info, pieces, rows, saved):
    att_t, inverse, first_row, key, value, weight, held = saved
    blocks = [shaped(n, TOK, 2 * HEAD_SIZE) for n in HELD]
    outs = pl.pallas_call(
        backward_kernel,
        in_specs=[SMEM] + [VMEM] * 14,
        out_specs=[VMEM] * 5,
        out_shape=[shaped(TOK, QROWS)] + blocks + blocks,
        scratch_shapes=[
            pltpu.VMEM((TOK, 8 * FEATURES), jnp.bfloat16),
            pltpu.VMEM((QROWS, TOK), jnp.float32),
            pltpu.VMEM((HEAD_SIZE, QROWS), jnp.bfloat16),
            pltpu.VMEM((QROWS, HEAD_SIZE), jnp.bfloat16),
            pltpu.VMEM((HEAD_SIZE, QROWS), jnp.float32),
            pltpu.VMEM((1, QROWS), jnp.float32),
            pltpu.VMEM((KEYS, 2 * HEAD_SIZE), jnp.bfloat16),
        ],
        compiler_params=params(BACKWARD_MIB),
        cost_estimate=cost(14_000_000_000, 1 << 20),
    )(info, held, *pieces, rows, key, value, weight, att_t, inverse, first_row)
    return outs[0], outs[1:3], outs[3:5]


def per_device(rotated_queries, rotated_keys, value_heads_packed, out_weight, out_cotangent, doc_ids):
    me = lax.axis_index("dp").astype(jnp.int32)
    z = lax.axis_index("tensor").astype(jnp.int32)
    info = jnp.stack([me // 2, me % 2, z])

    block = packed(rotated_keys, value_heads_packed, doc_ids)
    rows = rotated_queries.reshape(TOK, HEADS, HEAD_SIZE).transpose(1, 0, 2).reshape(QROWS, HEAD_SIZE)
    block_4 = chips_on(block, 4)
    block_8 = chips_on(block, 8)
    z_up, z_down, z_four = along_z(out_cotangent, -1), along_z(out_cotangent, 1), along_z(out_cotangent, 4)
    near = jnp.concatenate([block, block_4], 0)
    near, rows = lax.optimization_barrier((near, rows))
    own = [
        jnp.concatenate([near, block_8], 0),
        jnp.concatenate([chips_on(near, by) for by in (1, 2, 3)], 0),
    ]
    sib = [across(piece) for piece in own]
    z_far_up = along_z(jnp.concatenate([z_up, z_four], 0), -1)
    z_far_down = along_z(jnp.concatenate([z_down, z_four], 0), 1)

    saved, (to_up, to_down), (near_up, near_four, near_down, kept) = forward(
        info, out_weight, rows, own, sib
    )
    got_up = along_z(to_up, 1)
    got_down = along_z(to_down, -1)

    pieces = (z_far_up, z_far_down, z_up, z_four, z_down, out_cotangent)
    query_grad, grad_own, grad_sib = backward(info, pieces, rows, saved)

    grad_sib, got_up, got_down = lax.optimization_barrier((grad_sib, got_up, got_down))
    sum_up = along_z(low(near_up + wide(got_up[0])), 1)
    sum_four = along_z(low(near_four + wide(got_up[1]) + wide(got_down[1])), 4)
    sum_down = along_z(low(near_down + wide(got_down[0])), -1)
    projected = low(kept + wide(sum_up) + wide(sum_four) + wide(sum_down))

    both = [wide(mine) + wide(across(theirs)) for mine, theirs in zip(grad_own, grad_sib)]
    back = [wide(chips_on(low(both[1][2 * n : 2 * n + 2]), -(n + 1))) for n in range(3)]
    back_8 = wide(chips_on(low(both[0][2]), -8))
    near_sum = both[0][0:2] + back[0] + back[1] + back[2]
    total = near_sum[0] + back_8 + wide(chips_on(low(near_sum[1]), -4))
    total = low(total)
    return projected, query_grad, total[:, :HEAD_SIZE], total[:, HEAD_SIZE:]


def solution(mesh):
    return jax.shard_map(
        per_device,
        mesh=mesh,
        in_specs=(
            P("dp", "tensor"),
            P("dp", "tensor"),
            P("dp", "tensor"),
            P("tensor", None),
            P("dp", "tensor"),
            P("dp"),
        ),
        out_specs=(P("dp", "tensor"), P("dp", "tensor"), P("dp", "tensor"), P("dp", "tensor")),
        check_vma=False,
    )
```

```python
import math

import jax
import jax.numpy as jnp
from jax import lax
from jax.experimental import pallas as pl
from jax.experimental.pallas import tpu as pltpu
from jax.sharding import PartitionSpec as P

HEADS = 8
HEAD_SIZE = 128
TOK = 128
PAIR = 2 * TOK
DOCS = 16
ROWS = TOK + DOCS
SLOTS = 9
KEYS = SLOTS * PAIR
STEP = 2 * PAIR
CHUNK = 512
GRAD_CHUNK = 1024
QROWS = HEADS * TOK
FEATURES = 512
MASKED = -1e30
SCALE = 1.0 / math.sqrt(HEAD_SIZE)
SCALE_LOG2 = SCALE * math.log2(math.e)

VMEM = pl.BlockSpec(memory_space=pltpu.VMEM)
SMEM = pl.BlockSpec(memory_space=pltpu.SMEM)
HBM = pl.BlockSpec(memory_space=pltpu.HBM)
NT = (((1,), (1,)), ((), ()))

PLACE = {0: (0, 0), 4: (0, 1), 8: (0, 2), 1: (1, 0), 5: (1, 1), 2: (1, 2), 6: (1, 3), 3: (1, 4), 7: (1, 5)}
HELD = (3, 6)
PART_ORDER = (2, 5, 6, 3, 1, 4, 7, 0)
FORWARD_MIB = 34
BACKWARD_MIB = 12


def dot_nt(a, b):
    return lax.dot_general(a, b, NT, preferred_element_type=jnp.float32)


def dot(a, b):
    return jnp.dot(a, b, preferred_element_type=jnp.float32)


def params(mib):
    return pltpu.CompilerParams(vmem_limit_bytes=mib * 1024 * 1024)


def cost(flops, nbytes, trans=0):
    return pl.CostEstimate(flops=flops, bytes_accessed=nbytes, transcendentals=trans)


def shaped(*shape, dtype=jnp.bfloat16):
    return jax.ShapeDtypeStruct(shape, dtype)


def packed(keys, values, ids):
    numbers = jnp.broadcast_to(jnp.tile(ids, 2).astype(jnp.bfloat16)[None, :], (DOCS, 2 * TOK))
    return jnp.concatenate([jnp.concatenate([keys, values], 1), numbers], 0)[None]


def fetch_weight(aheads, z, w_ref, held_ref, sems):
    copies = []
    for n, ahead in enumerate(aheads):
        at = pl.multiple_of(lax.rem(z + ahead, 8) * FEATURES, FEATURES)
        copies.append(pltpu.make_async_copy(w_ref.at[:, pl.ds(at, FEATURES)], held_ref.at[:, pl.ds(n * FEATURES, FEATURES)], sems.at[n]))
    for copy in copies:
        copy.start()
    return copies


def bias_of(base, rows, core, query_pair, first_row):
    row = lax.broadcasted_iota(jnp.int32, (rows, TOK), 0)
    column = lax.broadcasted_iota(jnp.int32, (rows, TOK), 1)
    key_pos = base + jnp.where(row < PAIR, row, row - 2 * PAIR)
    query_pos = query_pair * PAIR + core * TOK + column
    allowed = (key_pos >= first_row) & (key_pos <= query_pos)
    bias = jnp.where(allowed, 0.0, MASKED)
    return jnp.concatenate([bias] * (CHUNK // TOK), 1)


def eights(value):
    return value.reshape(value.shape[0] // 8, 8, value.shape[1])


def forward_kernel(info_ref, w_ref, rows_ref, *refs):
    own, sib, refs = refs[:2], refs[2:4], refs[4:]
    att_t_ref, inverse_ref, first_ref, key_ref, value_ref, weight_ref, held_ref = refs[:7]
    sends, keeps, refs = refs[7:9], refs[9:13], refs[13:]
    score_ref, acc_ref, max_ref, sum_ref, att_ref, peak_ref, sems = refs
    query_pair, core = info_ref[0], info_ref[1]
    w_copies = fetch_weight(PART_ORDER, info_ref[2], w_ref, held_ref, sems)
    at_own = pl.multiple_of(core * TOK, TOK)
    at_sib = pl.multiple_of((1 - core) * TOK, TOK)
    number = lax.broadcasted_iota(jnp.int32, (DOCS, TOK), 0).astype(jnp.float32)
    below = jnp.zeros((DOCS, TOK), jnp.float32)
    for j in range(SLOTS):
        array, place = PLACE[j]
        valid = jnp.where(query_pair >= j, 1.0, 0.0)
        for held, at in ((own, at_own), (sib, at_sib)):
            ref = held[array]
            key_ref[pl.ds(j * PAIR + at, TOK), :] = ref[place, 0:TOK, 0:HEAD_SIZE]
            value_ref[pl.ds(j * PAIR + at, TOK), :] = ref[place, 0:TOK, HEAD_SIZE : 2 * HEAD_SIZE]
            ids = ref[place, TOK:ROWS, 0:TOK].astype(jnp.float32)
            below = below + jnp.where(ids < number, valid, 0.0)
    below = jnp.sum(below, axis=1, keepdims=True)
    mine = own[0][0, TOK:ROWS, 0:TOK].astype(jnp.float32)
    before = jnp.sum(jnp.where(mine == number, below, 0.0), axis=0, keepdims=True)
    first_row = before.astype(jnp.int32) + PAIR * jnp.maximum(query_pair - (SLOTS - 1), 0)
    first_ref[...] = first_row
    live = query_pair - jnp.min(first_row) // PAIR + 1
    max_ref[...] = jnp.full(max_ref.shape, MASKED, jnp.float32)
    sum_ref[...] = jnp.zeros(sum_ref.shape, jnp.float32)
    acc_ref[...] = jnp.zeros(acc_ref.shape, jnp.float32)

    def score_rows(start, count, base):
        rows = pl.ds(start, count)
        key = key_ref[rows, :]
        bias = bias_of(base, count, core, query_pair, first_row)
        for n in range(QROWS // CHUNK):
            cols = slice(n * CHUNK, (n + 1) * CHUNK)
            score = dot_nt(key, rows_ref[cols, :]) * SCALE_LOG2 + bias
            score_ref[rows, cols] = score
            max_ref[:, cols] = jnp.maximum(max_ref[:, cols], jnp.max(eights(score), axis=0))

    def mix_rows(start, count):
        rows = pl.ds(start, count)
        value_t = value_ref[rows, :].T
        for n in range(QROWS // CHUNK):
            cols = slice(n * CHUNK, (n + 1) * CHUNK)
            weight = jnp.exp2(score_ref[rows, cols] - peak_ref[:, cols])
            sum_ref[:, cols] = sum_ref[:, cols] + jnp.sum(eights(weight), axis=0)
            weight = weight.astype(jnp.bfloat16)
            weight_ref[rows, cols] = weight
            acc_ref[:, cols] = acc_ref[:, cols] + dot(value_t, weight)

    def score_step(s, unused):
        score_rows(pl.multiple_of(PAIR + s * STEP, PAIR), STEP, (query_pair - 1 - 2 * s) * PAIR)
        return unused

    def mix_step(s, unused):
        mix_rows(pl.multiple_of(PAIR + s * STEP, PAIR), STEP)
        return unused

    score_rows(0, PAIR, query_pair * PAIR)
    lax.fori_loop(0, live // 2, score_step, 0)
    peak_ref[...] = jnp.max(max_ref[...], axis=0, keepdims=True)
    mix_rows(0, PAIR)
    lax.fori_loop(0, live // 2, mix_step, 0)
    inverse = 1.0 / jnp.sum(sum_ref[...], axis=0, keepdims=True)
    inverse_ref[...] = inverse
    for h in range(HEADS):
        cols = slice(h * TOK, (h + 1) * TOK)
        mixed = acc_ref[:, cols] * inverse[:, cols]
        att_t_ref[:, cols] = mixed.astype(jnp.bfloat16)
        att_ref[:, h * HEAD_SIZE : (h + 1) * HEAD_SIZE] = mixed.T.astype(jnp.bfloat16)
    for copy in w_copies:
        copy.wait()
    for n in range(8):
        part = dot(att_ref[...], held_ref[:, n * FEATURES : (n + 1) * FEATURES])
        if n < 4:
            sends[n // 2][n % 2] = part.astype(jnp.bfloat16)
        else:
            keeps[n - 4][...] = part


def backward_kernel(info_ref, held_ref, *refs):
    pieces, refs = refs[:6], refs[6:]
    rows_ref, key_ref, value_ref, weight_ref, att_t_ref, inverse_ref, first_ref = refs[:7]
    dq_ref, own, sib, refs = refs[7], refs[8:10], refs[10:12], refs[12:]
    cot_ref, grad_ref, grad_t_ref, grows_ref, acc_ref, delta_ref, out_ref = refs
    query_pair, core = info_ref[0], info_ref[1]
    at_own = pl.multiple_of(core * TOK, TOK)
    at_sib = pl.multiple_of((1 - core) * TOK, TOK)
    live = query_pair - jnp.min(first_ref[...]) // PAIR + 1
    n = 0
    for ref in pieces:
        for j in range(ref.shape[0] // TOK):
            cot_ref[:, n * FEATURES : (n + 1) * FEATURES] = ref[j * TOK : (j + 1) * TOK, :]
            n = n + 1
    grad_ref[...] = dot_nt(cot_ref[...], held_ref[...])
    for h in range(HEADS):
        part = slice(h * TOK, (h + 1) * TOK)
        grad_t = grad_ref[:, part].T * inverse_ref[:, part]
        delta_ref[:, part] = jnp.sum(grad_t * att_t_ref[:, part].astype(jnp.float32), axis=0, keepdims=True)
        grad_t = grad_t.astype(jnp.bfloat16)
        grad_t_ref[:, part] = grad_t
        grows_ref[part, :] = grad_t.T
    acc_ref[...] = jnp.zeros(acc_ref.shape, jnp.float32)
    out_ref[...] = jnp.zeros(out_ref.shape, jnp.bfloat16)

    def grad_rows(start, count):
        rows = pl.ds(start, count)
        key_t = key_ref[rows, :].T
        value = value_ref[rows, :]
        dkey = jnp.zeros((count, HEAD_SIZE), jnp.float32)
        dvalue = jnp.zeros((count, HEAD_SIZE), jnp.float32)
        for n in range(QROWS // GRAD_CHUNK):
            cols = slice(n * GRAD_CHUNK, (n + 1) * GRAD_CHUNK)
            weight = weight_ref[rows, cols]
            gprob = dot(value, grad_t_ref[:, cols])
            gscore = (weight.astype(jnp.float32) * (gprob - delta_ref[:, cols])).astype(jnp.bfloat16)
            dvalue = dvalue + dot(weight, grows_ref[cols, :])
            dkey = dkey + dot(gscore, rows_ref[cols, :])
            acc_ref[:, cols] = acc_ref[:, cols] + dot(key_t, gscore)
        out_ref[rows, 0:HEAD_SIZE] = (dkey * SCALE).astype(jnp.bfloat16)
        out_ref[rows, HEAD_SIZE : 2 * HEAD_SIZE] = dvalue.astype(jnp.bfloat16)

    def grad_step(s, unused):
        grad_rows(pl.multiple_of(PAIR + s * STEP, PAIR), STEP)
        return unused

    grad_rows(0, PAIR)
    lax.fori_loop(0, live // 2, grad_step, 0)
    for j in range(SLOTS):
        array, place = PLACE[j]
        own[array][place] = out_ref[pl.ds(j * PAIR + at_own, TOK), :]
        sib[array][place] = out_ref[pl.ds(j * PAIR + at_sib, TOK), :]
    for h in range(HEADS):
        mixed = acc_ref[:, h * TOK : (h + 1) * TOK] * SCALE
        dq_ref[:, h * HEAD_SIZE : (h + 1) * HEAD_SIZE] = mixed.T.astype(jnp.bfloat16)


def chips_on(value, by):
    return lax.ppermute(value, "dp", [(i, (i + 2 * by) % 32) for i in range(32)])


def across(value):
    return lax.ppermute(value, "dp", [(i, i ^ 1) for i in range(32)])


def along_z(value, by):
    return lax.ppermute(value, "tensor", [(i, (i + by) % 8) for i in range(8)])


def wide(value):
    return value.astype(jnp.float32)


def low(value):
    return value.astype(jnp.bfloat16)


def forward(info, weight, rows, own, sib):
    outs = pl.pallas_call(
        forward_kernel,
        in_specs=[SMEM, HBM] + [VMEM] * 5,
        out_specs=[VMEM] * 13,
        out_shape=[
            shaped(HEAD_SIZE, QROWS),
            shaped(1, QROWS, dtype=jnp.float32),
            shaped(1, TOK, dtype=jnp.int32),
            shaped(KEYS, HEAD_SIZE),
            shaped(KEYS, HEAD_SIZE),
            shaped(KEYS, QROWS),
            shaped(QROWS, 8 * FEATURES),
        ]
        + [shaped(2, TOK, FEATURES)] * 2
        + [shaped(TOK, FEATURES, dtype=jnp.float32)] * 4,
        scratch_shapes=[
            pltpu.VMEM((KEYS, QROWS), jnp.float32),
            pltpu.VMEM((HEAD_SIZE, QROWS), jnp.float32),
            pltpu.VMEM((8, QROWS), jnp.float32),
            pltpu.VMEM((8, QROWS), jnp.float32),
            pltpu.VMEM((TOK, QROWS), jnp.bfloat16),
            pltpu.VMEM((1, QROWS), jnp.float32),
            pltpu.SemaphoreType.DMA((8,)),
        ],
        compiler_params=params(FORWARD_MIB),
        cost_estimate=cost(9_000_000_000, 1 << 20),
    )(info, weight, rows, *own, *sib)
    return outs[:7], outs[7:9], outs[9:]


def backward(info, pieces, rows, saved):
    att_t, inverse, first_row, key, value, weight, held = saved
    blocks = [shaped(n, TOK, 2 * HEAD_SIZE) for n in HELD]
    outs = pl.pallas_call(
        backward_kernel,
        in_specs=[SMEM] + [VMEM] * 14,
        out_specs=[VMEM] * 5,
        out_shape=[shaped(TOK, QROWS)] + blocks + blocks,
        scratch_shapes=[
            pltpu.VMEM((TOK, 8 * FEATURES), jnp.bfloat16),
            pltpu.VMEM((TOK, QROWS), jnp.float32),
            pltpu.VMEM((HEAD_SIZE, QROWS), jnp.bfloat16),
            pltpu.VMEM((QROWS, HEAD_SIZE), jnp.bfloat16),
            pltpu.VMEM((HEAD_SIZE, QROWS), jnp.float32),
            pltpu.VMEM((1, QROWS), jnp.float32),
            pltpu.VMEM((KEYS, 2 * HEAD_SIZE), jnp.bfloat16),
        ],
        compiler_params=params(BACKWARD_MIB),
        cost_estimate=cost(14_000_000_000, 1 << 20),
    )(info, held, *pieces, rows, key, value, weight, att_t, inverse, first_row)
    return outs[0], outs[1:3], outs[3:5]


def per_device(rotated_queries, rotated_keys, value_heads_packed, out_weight, out_cotangent, doc_ids):
    me = lax.axis_index("dp").astype(jnp.int32)
    z = lax.axis_index("tensor").astype(jnp.int32)
    info = jnp.stack([me // 2, me % 2, z])

    block = packed(rotated_keys, value_heads_packed, doc_ids)
    rows = rotated_queries.reshape(TOK, HEADS, HEAD_SIZE).transpose(1, 0, 2).reshape(QROWS, HEAD_SIZE)
    block_4 = chips_on(block, 4)
    block_8 = chips_on(block, 8)
    z_up, z_down, z_four = along_z(out_cotangent, -1), along_z(out_cotangent, 1), along_z(out_cotangent, 4)
    near = jnp.concatenate([block, block_4], 0)
    near, rows = lax.optimization_barrier((near, rows))
    own = [
        jnp.concatenate([near, block_8], 0),
        jnp.concatenate([chips_on(near, by) for by in (1, 2, 3)], 0),
    ]
    sib = [across(piece) for piece in own]
    z_far_up = along_z(jnp.concatenate([z_up, z_four], 0), -1)
    z_far_down = along_z(jnp.concatenate([z_down, z_four], 0), 1)

    saved, (to_up, to_down), (near_up, near_four, near_down, kept) = forward(
        info, out_weight, rows, own, sib
    )
    got_up = along_z(to_up, 1)
    got_down = along_z(to_down, -1)

    pieces = (z_far_up, z_far_down, z_up, z_four, z_down, out_cotangent)
    query_grad, grad_own, grad_sib = backward(info, pieces, rows, saved)

    grad_sib, got_up, got_down = lax.optimization_barrier((grad_sib, got_up, got_down))
    sum_up = along_z(low(near_up + wide(got_up[0])), 1)
    sum_four = along_z(low(near_four + wide(got_up[1]) + wide(got_down[1])), 4)
    sum_down = along_z(low(near_down + wide(got_down[0])), -1)
    projected = low(kept + wide(sum_up) + wide(sum_four) + wide(sum_down))

    both = [wide(mine) + wide(across(theirs)) for mine, theirs in zip(grad_own, grad_sib)]
    back = [wide(chips_on(low(both[1][2 * n : 2 * n + 2]), -(n + 1))) for n in range(3)]
    back_8 = wide(chips_on(low(both[0][2]), -8))
    near_sum = both[0][0:2] + back[0] + back[1] + back[2]
    total = near_sum[0] + back_8 + wide(chips_on(low(near_sum[1]), -4))
    total = low(total)
    return projected, query_grad, total[:, :HEAD_SIZE], total[:, HEAD_SIZE:]


def solution(mesh):
    return jax.shard_map(
        per_device,
        mesh=mesh,
        in_specs=(
            P("dp", "tensor"),
            P("dp", "tensor"),
            P("dp", "tensor"),
            P("tensor", None),
            P("dp", "tensor"),
            P("dp"),
        ),
        out_specs=(P("dp", "tensor"), P("dp", "tensor"), P("dp", "tensor"), P("dp", "tensor")),
        check_vma=False,
    )
```

```python
import math

import jax
import jax.numpy as jnp
from jax import lax
from jax.experimental import pallas as pl
from jax.experimental.pallas import tpu as pltpu
from jax.sharding import PartitionSpec as P

HEADS = 8
HEAD_SIZE = 128
TOK = 128
PAIR = 2 * TOK
DOCS = 16
ROWS = TOK + DOCS
SLOTS = 9
KEYS = SLOTS * PAIR
STEP = 2 * PAIR
CHUNK = 512
GRAD_CHUNK = 1024
QROWS = HEADS * TOK
FEATURES = 512
MASKED = -1e30
SCALE = 1.0 / math.sqrt(HEAD_SIZE)
SCALE_LOG2 = SCALE * math.log2(math.e)

VMEM = pl.BlockSpec(memory_space=pltpu.VMEM)
SMEM = pl.BlockSpec(memory_space=pltpu.SMEM)
HBM = pl.BlockSpec(memory_space=pltpu.HBM)
NT = (((1,), (1,)), ((), ()))

PLACE = {0: (0, 0), 4: (0, 1), 8: (0, 2), 1: (1, 0), 5: (1, 1), 2: (1, 2), 6: (1, 3), 3: (1, 4), 7: (1, 5)}
HELD = (3, 6)
PART_ORDER = (2, 5, 6, 3, 1, 4, 7, 0)
FORWARD_MIB = 34
BACKWARD_MIB = 12


def dot_nt(a, b):
    return lax.dot_general(a, b, NT, preferred_element_type=jnp.float32)


def dot(a, b):
    return jnp.dot(a, b, preferred_element_type=jnp.float32)


def params(mib):
    return pltpu.CompilerParams(vmem_limit_bytes=mib * 1024 * 1024)


def cost(flops, nbytes, trans=0):
    return pl.CostEstimate(flops=flops, bytes_accessed=nbytes, transcendentals=trans)


def shaped(*shape, dtype=jnp.bfloat16):
    return jax.ShapeDtypeStruct(shape, dtype)


def packed(keys, values, ids):
    numbers = jnp.broadcast_to(jnp.tile(ids, 2).astype(jnp.bfloat16)[None, :], (DOCS, 2 * TOK))
    return jnp.concatenate([jnp.concatenate([keys, values], 1), numbers], 0)[None]


def fetch_weight(aheads, z, w_ref, held_ref, sems):
    copies = []
    for n, ahead in enumerate(aheads):
        at = pl.multiple_of(lax.rem(z + ahead, 8) * FEATURES, FEATURES)
        copies.append(pltpu.make_async_copy(w_ref.at[:, pl.ds(at, FEATURES)], held_ref.at[:, pl.ds(n * FEATURES, FEATURES)], sems.at[n]))
    for copy in copies:
        copy.start()
    return copies


def bias_of(base, rows, core, query_pair, first_row):
    row = lax.broadcasted_iota(jnp.int32, (rows, TOK), 0)
    column = lax.broadcasted_iota(jnp.int32, (rows, TOK), 1)
    key_pos = base + jnp.where(row < PAIR, row, row - 2 * PAIR)
    query_pos = query_pair * PAIR + core * TOK + column
    allowed = (key_pos >= first_row) & (key_pos <= query_pos)
    bias = jnp.where(allowed, 0.0, MASKED)
    return jnp.concatenate([bias] * (CHUNK // TOK), 1)


def eights(value):
    return value.reshape(value.shape[0] // 8, 8, value.shape[1])


def forward_kernel(info_ref, w_ref, rows_ref, *refs):
    own, sib, refs = refs[:2], refs[2:4], refs[4:]
    att_t_ref, inverse_ref, first_ref, key_ref, value_ref, weight_ref, held_ref = refs[:7]
    sends, keeps, refs = refs[7:9], refs[9:13], refs[13:]
    score_ref, acc_ref, max_ref, sum_ref, att_ref, peak_ref, sems = refs
    query_pair, core = info_ref[0], info_ref[1]
    w_copies = fetch_weight(PART_ORDER, info_ref[2], w_ref, held_ref, sems)
    at_own = pl.multiple_of(core * TOK, TOK)
    at_sib = pl.multiple_of((1 - core) * TOK, TOK)
    number = lax.broadcasted_iota(jnp.int32, (DOCS, TOK), 0).astype(jnp.float32)
    below = jnp.zeros((DOCS, TOK), jnp.float32)
    for j in range(SLOTS):
        array, place = PLACE[j]
        valid = jnp.where(query_pair >= j, 1.0, 0.0)
        for held, at in ((own, at_own), (sib, at_sib)):
            ref = held[array]
            key_ref[pl.ds(j * PAIR + at, TOK), :] = ref[place, 0:TOK, 0:HEAD_SIZE]
            value_ref[pl.ds(j * PAIR + at, TOK), :] = ref[place, 0:TOK, HEAD_SIZE : 2 * HEAD_SIZE]
            ids = ref[place, TOK:ROWS, 0:TOK].astype(jnp.float32)
            below = below + jnp.where(ids < number, valid, 0.0)
    below = jnp.sum(below, axis=1, keepdims=True)
    mine = own[0][0, TOK:ROWS, 0:TOK].astype(jnp.float32)
    before = jnp.sum(jnp.where(mine == number, below, 0.0), axis=0, keepdims=True)
    first_row = before.astype(jnp.int32) + PAIR * jnp.maximum(query_pair - (SLOTS - 1), 0)
    first_ref[...] = first_row
    live = query_pair - jnp.min(first_row) // PAIR + 1
    max_ref[...] = jnp.full(max_ref.shape, MASKED, jnp.float32)
    sum_ref[...] = jnp.zeros(sum_ref.shape, jnp.float32)
    acc_ref[...] = jnp.zeros(acc_ref.shape, jnp.float32)

    def score_rows(start, count, base):
        rows = pl.ds(start, count)
        key = key_ref[rows, :]
        bias = bias_of(base, count, core, query_pair, first_row)
        for n in range(QROWS // CHUNK):
            cols = slice(n * CHUNK, (n + 1) * CHUNK)
            score = dot_nt(key, rows_ref[cols, :]) * SCALE_LOG2 + bias
            score_ref[rows, cols] = score
            max_ref[:, cols] = jnp.maximum(max_ref[:, cols], jnp.max(eights(score), axis=0))

    def mix_rows(start, count):
        rows = pl.ds(start, count)
        value_t = value_ref[rows, :].T
        for n in range(QROWS // CHUNK):
            cols = slice(n * CHUNK, (n + 1) * CHUNK)
            weight = jnp.exp2(score_ref[rows, cols] - peak_ref[:, cols])
            sum_ref[:, cols] = sum_ref[:, cols] + jnp.sum(eights(weight), axis=0)
            weight = weight.astype(jnp.bfloat16)
            weight_ref[rows, cols] = weight
            acc_ref[:, cols] = acc_ref[:, cols] + dot(value_t, weight)

    def score_step(s, unused):
        score_rows(pl.multiple_of(PAIR + s * STEP, PAIR), STEP, (query_pair - 1 - 2 * s) * PAIR)
        return unused

    def mix_step(s, unused):
        mix_rows(pl.multiple_of(PAIR + s * STEP, PAIR), STEP)
        return unused

    score_rows(0, PAIR, query_pair * PAIR)
    lax.fori_loop(0, live // 2, score_step, 0)
    peak_ref[...] = jnp.max(max_ref[...], axis=0, keepdims=True)
    mix_rows(0, PAIR)
    lax.fori_loop(0, live // 2, mix_step, 0)
    inverse = 1.0 / jnp.sum(sum_ref[...], axis=0, keepdims=True)
    inverse_ref[...] = inverse
    for h in range(HEADS):
        cols = slice(h * TOK, (h + 1) * TOK)
        mixed = acc_ref[:, cols] * inverse[:, cols]
        att_t_ref[:, cols] = mixed.astype(jnp.bfloat16)
        att_ref[:, h * HEAD_SIZE : (h + 1) * HEAD_SIZE] = mixed.T.astype(jnp.bfloat16)
    for copy in w_copies:
        copy.wait()
    for n in range(8):
        part = dot(att_ref[...], held_ref[:, n * FEATURES : (n + 1) * FEATURES])
        if n < 4:
            sends[n // 2][n % 2] = part.astype(jnp.bfloat16)
        else:
            keeps[n - 4][...] = part


def backward_kernel(info_ref, held_ref, *refs):
    pieces, refs = refs[:6], refs[6:]
    rows_ref, key_ref, value_ref, weight_ref, att_t_ref, inverse_ref, first_ref = refs[:7]
    dq_ref, own, sib, refs = refs[7], refs[8:10], refs[10:12], refs[12:]
    cot_ref, grad_ref, grad_t_ref, grows_ref, acc_ref, delta_ref, out_ref = refs
    query_pair, core = info_ref[0], info_ref[1]
    at_own = pl.multiple_of(core * TOK, TOK)
    at_sib = pl.multiple_of((1 - core) * TOK, TOK)
    live = query_pair - jnp.min(first_ref[...]) // PAIR + 1
    n = 0
    for ref in pieces:
        for j in range(ref.shape[0] // TOK):
            cot_ref[:, n * FEATURES : (n + 1) * FEATURES] = ref[j * TOK : (j + 1) * TOK, :]
            n = n + 1
    grad_ref[...] = dot_nt(cot_ref[...], held_ref[...])
    for h in range(HEADS):
        part = slice(h * TOK, (h + 1) * TOK)
        grad_t = grad_ref[:, part].T * inverse_ref[:, part]
        delta_ref[:, part] = jnp.sum(grad_t * att_t_ref[:, part].astype(jnp.float32), axis=0, keepdims=True)
        grad_t = grad_t.astype(jnp.bfloat16)
        grad_t_ref[:, part] = grad_t
        grows_ref[part, :] = grad_t.T
    acc_ref[...] = jnp.zeros(acc_ref.shape, jnp.float32)
    out_ref[...] = jnp.zeros(out_ref.shape, jnp.bfloat16)

    def grad_rows(start, count):
        rows = pl.ds(start, count)
        key_t = key_ref[rows, :].T
        value = value_ref[rows, :]
        dkey = jnp.zeros((count, HEAD_SIZE), jnp.float32)
        dvalue = jnp.zeros((count, HEAD_SIZE), jnp.float32)
        for n in range(QROWS // GRAD_CHUNK):
            cols = slice(n * GRAD_CHUNK, (n + 1) * GRAD_CHUNK)
            weight = weight_ref[rows, cols]
            gprob = dot(value, grad_t_ref[:, cols])
            gscore = (weight.astype(jnp.float32) * (gprob - delta_ref[:, cols])).astype(jnp.bfloat16)
            dvalue = dvalue + dot(weight, grows_ref[cols, :])
            dkey = dkey + dot(gscore, rows_ref[cols, :])
            acc_ref[:, cols] = acc_ref[:, cols] + dot(key_t, gscore)
        out_ref[rows, 0:HEAD_SIZE] = (dkey * SCALE).astype(jnp.bfloat16)
        out_ref[rows, HEAD_SIZE : 2 * HEAD_SIZE] = dvalue.astype(jnp.bfloat16)

    def grad_step(s, unused):
        grad_rows(pl.multiple_of(PAIR + s * STEP, PAIR), STEP)
        return unused

    grad_rows(0, PAIR)
    lax.fori_loop(0, live // 2, grad_step, 0)
    for j in range(SLOTS):
        array, place = PLACE[j]
        own[array][place] = out_ref[pl.ds(j * PAIR + at_own, TOK), :]
        sib[array][place] = out_ref[pl.ds(j * PAIR + at_sib, TOK), :]
    for h in range(HEADS):
        mixed = acc_ref[:, h * TOK : (h + 1) * TOK] * SCALE
        dq_ref[:, h * HEAD_SIZE : (h + 1) * HEAD_SIZE] = mixed.T.astype(jnp.bfloat16)


def chips_on(value, by):
    return lax.ppermute(value, "dp", [(i, (i + 2 * by) % 32) for i in range(32)])


def across(value):
    return lax.ppermute(value, "dp", [(i, i ^ 1) for i in range(32)])


def along_z(value, by):
    return lax.ppermute(value, "tensor", [(i, (i + by) % 8) for i in range(8)])


def wide(value):
    return value.astype(jnp.float32)


def low(value):
    return value.astype(jnp.bfloat16)


def forward(info, weight, rows, own, sib):
    outs = pl.pallas_call(
        forward_kernel,
        in_specs=[SMEM, HBM] + [VMEM] * 5,
        out_specs=[VMEM] * 13,
        out_shape=[
            shaped(HEAD_SIZE, QROWS),
            shaped(1, QROWS, dtype=jnp.float32),
            shaped(1, TOK, dtype=jnp.int32),
            shaped(KEYS, HEAD_SIZE),
            shaped(KEYS, HEAD_SIZE),
            shaped(KEYS, QROWS),
            shaped(QROWS, 8 * FEATURES),
        ]
        + [shaped(2, TOK, FEATURES)] * 2
        + [shaped(TOK, FEATURES, dtype=jnp.float32)] * 4,
        scratch_shapes=[
            pltpu.VMEM((KEYS, QROWS), jnp.float32),
            pltpu.VMEM((HEAD_SIZE, QROWS), jnp.float32),
            pltpu.VMEM((8, QROWS), jnp.float32),
            pltpu.VMEM((8, QROWS), jnp.float32),
            pltpu.VMEM((TOK, QROWS), jnp.bfloat16),
            pltpu.VMEM((1, QROWS), jnp.float32),
            pltpu.SemaphoreType.DMA((8,)),
        ],
        compiler_params=params(FORWARD_MIB),
        cost_estimate=cost(9_000_000_000, 1 << 20),
    )(info, weight, rows, *own, *sib)
    return outs[:7], outs[7:9], outs[9:]


def backward(info, pieces, rows, saved):
    att_t, inverse, first_row, key, value, weight, held = saved
    blocks = [shaped(n, TOK, 2 * HEAD_SIZE) for n in HELD]
    outs = pl.pallas_call(
        backward_kernel,
        in_specs=[SMEM] + [VMEM] * 14,
        out_specs=[VMEM] * 5,
        out_shape=[shaped(TOK, QROWS)] + blocks + blocks,
        scratch_shapes=[
            pltpu.VMEM((TOK, 8 * FEATURES), jnp.bfloat16),
            pltpu.VMEM((TOK, QROWS), jnp.float32),
            pltpu.VMEM((HEAD_SIZE, QROWS), jnp.bfloat16),
            pltpu.VMEM((QROWS, HEAD_SIZE), jnp.bfloat16),
            pltpu.VMEM((HEAD_SIZE, QROWS), jnp.float32),
            pltpu.VMEM((1, QROWS), jnp.float32),
            pltpu.VMEM((KEYS, 2 * HEAD_SIZE), jnp.bfloat16),
        ],
        compiler_params=params(BACKWARD_MIB),
        cost_estimate=cost(14_000_000_000, 1 << 20),
    )(info, held, *pieces, rows, key, value, weight, att_t, inverse, first_row)
    return outs[0], outs[1:3], outs[3:5]


def per_device(rotated_queries, rotated_keys, value_heads_packed, out_weight, out_cotangent, doc_ids):
    me = lax.axis_index("dp").astype(jnp.int32)
    z = lax.axis_index("tensor").astype(jnp.int32)
    info = jnp.stack([me // 2, me % 2, z])

    block = packed(rotated_keys, value_heads_packed, doc_ids)
    rows = rotated_queries.reshape(TOK, HEADS, HEAD_SIZE).transpose(1, 0, 2).reshape(QROWS, HEAD_SIZE)
    block_4 = chips_on(block, 4)
    block_8 = chips_on(block, 8)
    z_up, z_down, z_four = along_z(out_cotangent, -1), along_z(out_cotangent, 1), along_z(out_cotangent, 4)
    near = jnp.concatenate([block, block_4], 0)
    near, rows = lax.optimization_barrier((near, rows))
    own = [
        jnp.concatenate([near, block_8], 0),
        jnp.concatenate([chips_on(near, by) for by in (1, 2, 3)], 0),
    ]
    sib = [across(piece) for piece in own]
    z_far_up = along_z(jnp.concatenate([z_up, z_four], 0), -1)
    z_far_down = along_z(jnp.concatenate([z_down, z_four], 0), 1)

    saved, (to_up, to_down), (near_up, near_four, near_down, kept) = forward(
        info, out_weight, rows, own, sib
    )
    got_up = along_z(to_up, 1)
    got_down = along_z(to_down, -1)

    pieces = (z_far_up, z_far_down, z_up, z_four, z_down, out_cotangent)
    query_grad, grad_own, grad_sib = backward(info, pieces, rows, saved)

    grad_sib, got_up, got_down = lax.optimization_barrier((grad_sib, got_up, got_down))
    sum_up = along_z(low(near_up + wide(got_up[0])), 1)
    sum_four = along_z(low(near_four + wide(got_up[1]) + wide(got_down[1])), 4)
    sum_down = along_z(low(near_down + wide(got_down[0])), -1)

    both = [wide(mine) + wide(across(theirs)) for mine, theirs in zip(grad_own, grad_sib)]
    back = [chips_on(low(both[1][2 * n : 2 * n + 2]), -(n + 1)) for n in range(3)]
    back, sum_up, sum_down = lax.optimization_barrier((back, sum_up, sum_down))
    back = [wide(value) for value in back]
    back_8 = wide(chips_on(low(both[0][2]), -8))
    near_sum = both[0][0:2] + back[0] + back[1] + back[2]
    total = near_sum[0] + back_8 + wide(chips_on(low(near_sum[1]), -4))
    total = low(total)
    projected = low(kept + wide(sum_up) + wide(sum_four) + wide(sum_down))
    return projected, query_grad, total[:, :HEAD_SIZE], total[:, HEAD_SIZE:]


def solution(mesh):
    return jax.shard_map(
        per_device,
        mesh=mesh,
        in_specs=(
            P("dp", "tensor"),
            P("dp", "tensor"),
            P("dp", "tensor"),
            P("tensor", None),
            P("dp", "tensor"),
            P("dp"),
        ),
        out_specs=(P("dp", "tensor"), P("dp", "tensor"), P("dp", "tensor"), P("dp", "tensor")),
        check_vma=False,
    )
```

```python
import math

import jax
import jax.numpy as jnp
from jax import lax
from jax.experimental import pallas as pl
from jax.experimental.pallas import tpu as pltpu
from jax.sharding import PartitionSpec as P

HEADS = 8
HEAD_SIZE = 128
TOK = 128
PAIR = 2 * TOK
DOCS = 16
ROWS = TOK + DOCS
SLOTS = 9
KEYS = SLOTS * PAIR
STEP = 2 * PAIR
CHUNK = 512
GRAD_CHUNK = 1024
QROWS = HEADS * TOK
FEATURES = 512
MASKED = -1e30
SCALE = 1.0 / math.sqrt(HEAD_SIZE)
SCALE_LOG2 = SCALE * math.log2(math.e)

VMEM = pl.BlockSpec(memory_space=pltpu.VMEM)
SMEM = pl.BlockSpec(memory_space=pltpu.SMEM)
HBM = pl.BlockSpec(memory_space=pltpu.HBM)
NT = (((1,), (1,)), ((), ()))

PLACE = {0: (0, 0), 4: (0, 1), 8: (0, 2), 1: (1, 0), 5: (1, 1), 2: (1, 2), 6: (1, 3), 3: (1, 4), 7: (1, 5)}
HELD = (3, 6)
PART_ORDER = (2, 5, 6, 3, 1, 4, 7, 0)
FORWARD_MIB = 34
BACKWARD_MIB = 12


def dot_nt(a, b):
    return lax.dot_general(a, b, NT, preferred_element_type=jnp.float32)


def dot(a, b):
    return jnp.dot(a, b, preferred_element_type=jnp.float32)


def params(mib):
    return pltpu.CompilerParams(vmem_limit_bytes=mib * 1024 * 1024)


def cost(flops, nbytes, trans=0):
    return pl.CostEstimate(flops=flops, bytes_accessed=nbytes, transcendentals=trans)


def shaped(*shape, dtype=jnp.bfloat16):
    return jax.ShapeDtypeStruct(shape, dtype)


def packed(keys, values, ids):
    numbers = jnp.broadcast_to(jnp.tile(ids, 2).astype(jnp.bfloat16)[None, :], (DOCS, 2 * TOK))
    return jnp.concatenate([jnp.concatenate([keys, values], 1), numbers], 0)[None]


def fetch_weight(aheads, z, w_ref, held_ref, sems):
    copies = []
    for n, ahead in enumerate(aheads):
        at = pl.multiple_of(lax.rem(z + ahead, 8) * FEATURES, FEATURES)
        copies.append(pltpu.make_async_copy(w_ref.at[:, pl.ds(at, FEATURES)], held_ref.at[:, pl.ds(n * FEATURES, FEATURES)], sems.at[n]))
    for copy in copies:
        copy.start()
    return copies


def bias_of(base, rows, core, query_pair, first_row):
    row = lax.broadcasted_iota(jnp.int32, (rows, TOK), 0)
    column = lax.broadcasted_iota(jnp.int32, (rows, TOK), 1)
    key_pos = base + jnp.where(row < PAIR, row, row - 2 * PAIR)
    query_pos = query_pair * PAIR + core * TOK + column
    allowed = (key_pos >= first_row) & (key_pos <= query_pos)
    bias = jnp.where(allowed, 0.0, MASKED)
    return jnp.concatenate([bias] * (CHUNK // TOK), 1)


def eights(value):
    return value.reshape(value.shape[0] // 8, 8, value.shape[1])


def forward_kernel(info_ref, w_ref, rows_ref, *refs):
    own, sib, refs = refs[:2], refs[2:4], refs[4:]
    att_t_ref, inverse_ref, first_ref, key_ref, value_ref, weight_ref, held_ref = refs[:7]
    sends, keeps, refs = refs[7:9], refs[9:13], refs[13:]
    score_ref, acc_ref, max_ref, sum_ref, att_ref, peak_ref, sems = refs
    query_pair, core = info_ref[0], info_ref[1]
    w_copies = fetch_weight(PART_ORDER, info_ref[2], w_ref, held_ref, sems)
    at_own = pl.multiple_of(core * TOK, TOK)
    at_sib = pl.multiple_of((1 - core) * TOK, TOK)
    number = lax.broadcasted_iota(jnp.int32, (DOCS, TOK), 0).astype(jnp.float32)
    below = jnp.zeros((DOCS, TOK), jnp.float32)
    for j in range(SLOTS):
        array, place = PLACE[j]
        valid = jnp.where(query_pair >= j, 1.0, 0.0)
        for held, at in ((own, at_own), (sib, at_sib)):
            ref = held[array]
            key_ref[pl.ds(j * PAIR + at, TOK), :] = ref[place, 0:TOK, 0:HEAD_SIZE]
            value_ref[pl.ds(j * PAIR + at, TOK), :] = ref[place, 0:TOK, HEAD_SIZE : 2 * HEAD_SIZE]
            ids = ref[place, TOK:ROWS, 0:TOK].astype(jnp.float32)
            below = below + jnp.where(ids < number, valid, 0.0)
    below = jnp.sum(below, axis=1, keepdims=True)
    mine = own[0][0, TOK:ROWS, 0:TOK].astype(jnp.float32)
    before = jnp.sum(jnp.where(mine == number, below, 0.0), axis=0, keepdims=True)
    first_row = before.astype(jnp.int32) + PAIR * jnp.maximum(query_pair - (SLOTS - 1), 0)
    first_ref[...] = first_row
    live = query_pair - jnp.min(first_row) // PAIR + 1
    max_ref[...] = jnp.full(max_ref.shape, MASKED, jnp.float32)
    sum_ref[...] = jnp.zeros(sum_ref.shape, jnp.float32)
    acc_ref[...] = jnp.zeros(acc_ref.shape, jnp.float32)

    def score_rows(start, count, base):
        rows = pl.ds(start, count)
        key = key_ref[rows, :]
        bias = bias_of(base, count, core, query_pair, first_row)
        for n in range(QROWS // CHUNK):
            cols = slice(n * CHUNK, (n + 1) * CHUNK)
            score = dot_nt(key, rows_ref[cols, :]) * SCALE_LOG2 + bias
            score_ref[rows, cols] = score
            max_ref[:, cols] = jnp.maximum(max_ref[:, cols], jnp.max(eights(score), axis=0))

    def mix_rows(start, count):
        rows = pl.ds(start, count)
        value_t = value_ref[rows, :].T
        for n in range(QROWS // CHUNK):
            cols = slice(n * CHUNK, (n + 1) * CHUNK)
            weight = jnp.exp2(score_ref[rows, cols] - peak_ref[:, cols])
            sum_ref[:, cols] = sum_ref[:, cols] + jnp.sum(eights(weight), axis=0)
            weight = weight.astype(jnp.bfloat16)
            weight_ref[rows, cols] = weight
            acc_ref[:, cols] = acc_ref[:, cols] + dot(value_t, weight)

    def score_step(s, unused):
        score_rows(pl.multiple_of(PAIR + s * STEP, PAIR), STEP, (query_pair - 1 - 2 * s) * PAIR)
        return unused

    def mix_step(s, unused):
        mix_rows(pl.multiple_of(PAIR + s * STEP, PAIR), STEP)
        return unused

    score_rows(0, PAIR, query_pair * PAIR)
    lax.fori_loop(0, live // 2, score_step, 0)
    peak_ref[...] = jnp.max(max_ref[...], axis=0, keepdims=True)
    mix_rows(0, PAIR)
    lax.fori_loop(0, live // 2, mix_step, 0)
    inverse = 1.0 / jnp.sum(sum_ref[...], axis=0, keepdims=True)
    inverse_ref[...] = inverse
    for h in range(HEADS):
        cols = slice(h * TOK, (h + 1) * TOK)
        mixed = acc_ref[:, cols] * inverse[:, cols]
        att_t_ref[:, cols] = mixed.astype(jnp.bfloat16)
        att_ref[:, h * HEAD_SIZE : (h + 1) * HEAD_SIZE] = mixed.T.astype(jnp.bfloat16)
    for copy in w_copies:
        copy.wait()
    for n in range(8):
        part = dot(att_ref[...], held_ref[:, n * FEATURES : (n + 1) * FEATURES])
        if n < 4:
            sends[n // 2][n % 2] = part.astype(jnp.bfloat16)
        else:
            keeps[n - 4][...] = part


def backward_kernel(info_ref, held_ref, *refs):
    pieces, refs = refs[:6], refs[6:]
    rows_ref, key_ref, value_ref, weight_ref, att_t_ref, inverse_ref, first_ref = refs[:7]
    dq_ref, own, sib, refs = refs[7], refs[8:10], refs[10:12], refs[12:]
    cot_ref, grad_ref, grad_t_ref, grows_ref, acc_ref, delta_ref, out_ref = refs
    query_pair, core = info_ref[0], info_ref[1]
    at_own = pl.multiple_of(core * TOK, TOK)
    at_sib = pl.multiple_of((1 - core) * TOK, TOK)
    live = query_pair - jnp.min(first_ref[...]) // PAIR + 1
    n = 0
    for ref in pieces:
        for j in range(ref.shape[0] // TOK):
            cot_ref[:, n * FEATURES : (n + 1) * FEATURES] = ref[j * TOK : (j + 1) * TOK, :]
            n = n + 1
    grad_ref[...] = dot_nt(cot_ref[...], held_ref[...])
    for h in range(HEADS):
        part = slice(h * TOK, (h + 1) * TOK)
        grad_t = grad_ref[:, part].T * inverse_ref[:, part]
        delta_ref[:, part] = jnp.sum(grad_t * att_t_ref[:, part].astype(jnp.float32), axis=0, keepdims=True)
        grad_t = grad_t.astype(jnp.bfloat16)
        grad_t_ref[:, part] = grad_t
        grows_ref[part, :] = grad_t.T
    acc_ref[...] = jnp.zeros(acc_ref.shape, jnp.float32)
    out_ref[...] = jnp.zeros(out_ref.shape, jnp.bfloat16)

    def grad_rows(start, count):
        rows = pl.ds(start, count)
        key_t = key_ref[rows, :].T
        value = value_ref[rows, :]
        dkey = jnp.zeros((count, HEAD_SIZE), jnp.float32)
        dvalue = jnp.zeros((count, HEAD_SIZE), jnp.float32)
        for n in range(QROWS // GRAD_CHUNK):
            cols = slice(n * GRAD_CHUNK, (n + 1) * GRAD_CHUNK)
            weight = weight_ref[rows, cols]
            gprob = dot(value, grad_t_ref[:, cols])
            gscore = (weight.astype(jnp.float32) * (gprob - delta_ref[:, cols])).astype(jnp.bfloat16)
            dvalue = dvalue + dot(weight, grows_ref[cols, :])
            dkey = dkey + dot(gscore, rows_ref[cols, :])
            acc_ref[:, cols] = acc_ref[:, cols] + dot(key_t, gscore)
        out_ref[rows, 0:HEAD_SIZE] = (dkey * SCALE).astype(jnp.bfloat16)
        out_ref[rows, HEAD_SIZE : 2 * HEAD_SIZE] = dvalue.astype(jnp.bfloat16)

    def grad_step(s, unused):
        grad_rows(pl.multiple_of(PAIR + s * STEP, PAIR), STEP)
        return unused

    grad_rows(0, PAIR)
    lax.fori_loop(0, live // 2, grad_step, 0)
    for j in range(SLOTS):
        array, place = PLACE[j]
        own[array][place] = out_ref[pl.ds(j * PAIR + at_own, TOK), :]
        sib[array][place] = out_ref[pl.ds(j * PAIR + at_sib, TOK), :]
    for h in range(HEADS):
        mixed = acc_ref[:, h * TOK : (h + 1) * TOK] * SCALE
        dq_ref[:, h * HEAD_SIZE : (h + 1) * HEAD_SIZE] = mixed.T.astype(jnp.bfloat16)


def chips_on(value, by):
    return lax.ppermute(value, "dp", [(i, (i + 2 * by) % 32) for i in range(32)])


def across(value):
    return lax.ppermute(value, "dp", [(i, i ^ 1) for i in range(32)])


def along_z(value, by):
    return lax.ppermute(value, "tensor", [(i, (i + by) % 8) for i in range(8)])


def wide(value):
    return value.astype(jnp.float32)


def low(value):
    return value.astype(jnp.bfloat16)


def forward(info, weight, rows, own, sib):
    outs = pl.pallas_call(
        forward_kernel,
        in_specs=[SMEM, HBM] + [VMEM] * 5,
        out_specs=[VMEM] * 13,
        out_shape=[
            shaped(HEAD_SIZE, QROWS),
            shaped(1, QROWS, dtype=jnp.float32),
            shaped(1, TOK, dtype=jnp.int32),
            shaped(KEYS, HEAD_SIZE),
            shaped(KEYS, HEAD_SIZE),
            shaped(KEYS, QROWS),
            shaped(QROWS, 8 * FEATURES),
        ]
        + [shaped(2, TOK, FEATURES)] * 2
        + [shaped(TOK, FEATURES, dtype=jnp.float32)] * 4,
        scratch_shapes=[
            pltpu.VMEM((KEYS, QROWS), jnp.float32),
            pltpu.VMEM((HEAD_SIZE, QROWS), jnp.float32),
            pltpu.VMEM((8, QROWS), jnp.float32),
            pltpu.VMEM((8, QROWS), jnp.float32),
            pltpu.VMEM((TOK, QROWS), jnp.bfloat16),
            pltpu.VMEM((1, QROWS), jnp.float32),
            pltpu.SemaphoreType.DMA((8,)),
        ],
        compiler_params=params(FORWARD_MIB),
        cost_estimate=cost(9_000_000_000, 1 << 20),
    )(info, weight, rows, *own, *sib)
    return outs[:7], outs[7:9], outs[9:]


def backward(info, pieces, rows, saved):
    att_t, inverse, first_row, key, value, weight, held = saved
    blocks = [shaped(n, TOK, 2 * HEAD_SIZE) for n in HELD]
    outs = pl.pallas_call(
        backward_kernel,
        in_specs=[SMEM] + [VMEM] * 14,
        out_specs=[VMEM] * 5,
        out_shape=[shaped(TOK, QROWS)] + blocks + blocks,
        scratch_shapes=[
            pltpu.VMEM((TOK, 8 * FEATURES), jnp.bfloat16),
            pltpu.VMEM((TOK, QROWS), jnp.float32),
            pltpu.VMEM((HEAD_SIZE, QROWS), jnp.bfloat16),
            pltpu.VMEM((QROWS, HEAD_SIZE), jnp.bfloat16),
            pltpu.VMEM((HEAD_SIZE, QROWS), jnp.float32),
            pltpu.VMEM((1, QROWS), jnp.float32),
            pltpu.VMEM((KEYS, 2 * HEAD_SIZE), jnp.bfloat16),
        ],
        compiler_params=params(BACKWARD_MIB),
        cost_estimate=cost(14_000_000_000, 1 << 20),
    )(info, held, *pieces, rows, key, value, weight, att_t, inverse, first_row)
    return outs[0], outs[1:3], outs[3:5]


def per_device(rotated_queries, rotated_keys, value_heads_packed, out_weight, out_cotangent, doc_ids):
    me = lax.axis_index("dp").astype(jnp.int32)
    z = lax.axis_index("tensor").astype(jnp.int32)
    info = jnp.stack([me // 2, me % 2, z])

    block = packed(rotated_keys, value_heads_packed, doc_ids)
    rows = rotated_queries.reshape(TOK, HEADS, HEAD_SIZE).transpose(1, 0, 2).reshape(QROWS, HEAD_SIZE)
    block_4 = chips_on(block, 4)
    block_8 = chips_on(block, 8)
    z_up, z_down, z_four = along_z(out_cotangent, -1), along_z(out_cotangent, 1), along_z(out_cotangent, 4)
    near = jnp.concatenate([block, block_4], 0)
    near, rows = lax.optimization_barrier((near, rows))
    own = [
        jnp.concatenate([near, block_8], 0),
        jnp.concatenate([chips_on(near, by) for by in (1, 2, 3)], 0),
    ]
    sib = [across(piece) for piece in own]
    z_far_up = along_z(jnp.concatenate([z_up, z_four], 0), -1)
    z_far_down = along_z(jnp.concatenate([z_down, z_four], 0), 1)

    saved, (to_up, to_down), (near_up, near_four, near_down, kept) = forward(
        info, out_weight, rows, own, sib
    )
    got_up = along_z(to_up, 1)
    got_down = along_z(to_down, -1)

    pieces = (z_far_up, z_far_down, z_up, z_four, z_down, out_cotangent)
    query_grad, grad_own, grad_sib = backward(info, pieces, rows, saved)

    grad_sib, got_up, got_down = lax.optimization_barrier((grad_sib, got_up, got_down))
    sum_up = along_z(low(near_up + wide(got_up[0])), 1)
    sum_four = along_z(low(near_four + wide(got_up[1]) + wide(got_down[1])), 4)
    sum_down = along_z(low(near_down + wide(got_down[0])), -1)

    both = [wide(mine) + wide(across(theirs)) for mine, theirs in zip(grad_own, grad_sib)]
    back = [chips_on(low(both[1][2 * n : 2 * n + 2]), -(n + 1)) for n in range(3)]
    back, sum_down = lax.optimization_barrier((back, sum_down))
    back = [wide(value) for value in back]
    back_8 = wide(chips_on(low(both[0][2]), -8))
    near_sum = both[0][0:2] + back[0] + back[1] + back[2]
    total = near_sum[0] + back_8 + wide(chips_on(low(near_sum[1]), -4))
    total = low(total)
    projected = low(kept + wide(sum_up) + wide(sum_four) + wide(sum_down))
    return projected, query_grad, total[:, :HEAD_SIZE], total[:, HEAD_SIZE:]


def solution(mesh):
    return jax.shard_map(
        per_device,
        mesh=mesh,
        in_specs=(
            P("dp", "tensor"),
            P("dp", "tensor"),
            P("dp", "tensor"),
            P("tensor", None),
            P("dp", "tensor"),
            P("dp"),
        ),
        out_specs=(P("dp", "tensor"), P("dp", "tensor"), P("dp", "tensor"), P("dp", "tensor")),
        check_vma=False,
    )
```
